256 devices in a mesh: base: 32 (over x, y, core), band: 8 (over z).
Axes of the slice: x: 4, y: 4, z: 8, core: 2. Of those that a mesh axis runs over, the one named last changes fastest.
Arguments:
- visibilities: float32 [65536, 2, 128], P(('base', 'band')), may hold values from -6 to 6
- coords: float32 [65536, 2, 8], P(('base', 'band')), may hold values from -11.2 to 11.2
- chan_scale: float32 [16], replicated, may hold values from 0.9 to 1.1
- taper_gain: float32 [32, 32], replicated, may hold values from 0.25 to 1
- owner_base: int32 [65536, 1], P(('base', 'band')), may hold values from 0 to 31; in each aligned block of 256 rows (0 to 255, 256 to 511, ...) at most 16 rows name the same one
- tile_cell: int32 [65536], P(('base', 'band')), may hold values from 0 to 255
Outputs:
- image: float32 [2, 8192, 8192], P(None, ('base', 'band'))
The draws below stay inside these ranges and needn't reach their ends.
Inputs may be any that keep to these rules, and one draw needn't show every extreme that they name: `owner_base`: among the 256 baselines of one device no value occurs more than 16 times, and in every draw some device has a value exactly 16 times.
All inputs are finite; a program needn't handle non-finite values.
Results may differ from the reference program's by a relative error of at most 0.0003.
Values sent between devices are 32-bit elements; how exact they have to be, the bound alone decides.
A program may use at most 128 MiB of HBM per device.

```python
import math
import jax
import jax.numpy as jnp
import numpy as np
from jax import lax

G = 8192
TILE = 32
TIMES = 8
CHANS = 16
SLOT_DEV = 256
CAP = 16
TPR = 32
TPC = 8
SLOTS = 65536
N_BASE = 32
N_BAND = 8
DEVICES = 256


def set_ends(entries, own_key, smallest, largest):
    longest = entries.shape.index(max(entries.shape))
    spots = []
    for shift in (0, 1):
        where = [jax.random.randint(jax.random.fold_in(own_key, axis), (), 0, length) for axis, length in enumerate(entries.shape)]
        where[longest] = (where[longest] + shift) % entries.shape[longest]
        spots.append(tuple(where))
    return entries.at[spots[0]].set(smallest).at[spots[1]].set(largest)


def steps_of(own_key, shape, split, low, high):
    def one(dim, blocks):
        steps = jax.random.uniform(jax.random.fold_in(jax.random.fold_in(own_key, 6), dim), (blocks,), jnp.float32, low / len(split), high / len(split))
        return jnp.repeat(jnp.exp(steps), shape[dim] // blocks).reshape((-1,) + (1,) * (len(shape) - dim - 1))

    loudness = one(*split[0])
    for cut in split[1:]:
        loudness = loudness * one(*cut)
    return loudness


def deal_out(key, own, number, rows, count, top, bound, skew):
    sequence = jax.random.permutation(key, count)
    heavy_load, ordinary = load_shares(count, rows * top, bound, skew, True), load_shares(count, rows * top, bound, skew, False)
    places = jnp.arange(count)

    def named(tallies, turn):
        used = int((tallies > 0).sum())
        fixed = max(1, used // 4)
        shifted = fixed + (places - fixed + turn * (used - fixed)) % max(1, count - fixed)
        return jnp.zeros((count,), jnp.int32).at[sequence[jnp.where(places < fixed, places, shifted)]].set(jnp.asarray(tallies, jnp.int32))

    tallies = jnp.where(number % 4 == 0, named(heavy_load, number // 4), named(ordinary, number - number // 4 - 1))
    mixed = jax.random.permutation(jax.random.fold_in(own, 3), count)
    giver, sink = mixed[0:count // 2 * 2:2], mixed[1:count // 2 * 2:2]
    margin = jnp.minimum(tallies[giver] - 1, bound - tallies[sink]) // 2
    margin = jnp.where((giver == sequence[0]) | (sink == sequence[0]) | (tallies[sink] == 0), 0, jnp.maximum(margin, 0))
    shifted = jax.random.randint(jax.random.fold_in(own, 4), (count // 2,), 0, 1 << 20) % (margin + 1)
    tallies = tallies.at[giver].add(-shifted).at[sink].add(shifted)
    members = jnp.searchsorted(jnp.cumsum(tallies), jnp.arange(rows * top), side="right").astype(jnp.int32)
    grid = members.reshape(top, rows).T
    grid = grid[jax.random.permutation(jax.random.fold_in(own, 1), rows)]
    turn = jax.random.randint(jax.random.fold_in(own, 2), (rows, 1), 0, top)
    return jnp.take_along_axis(grid, (jnp.arange(top)[None, :] + turn) % top, axis=1)


def load_shares(count, total, bound, lean, full):
    portions = [(1 << 20) // math.isqrt(rank ** lean) + 1 for rank in range(1, count + 1)]
    largest = bound if full else min(bound, max(-(-total // count), total * portions[0] // sum(portions)))
    least = 1 if total - largest >= count - 1 else 0
    counts, surplus = [largest] + [least] * (count - 1), total - largest - least * (count - 1)
    while surplus > 0:
        free = [i for i in range(1, count) if counts[i] < largest] or [i for i in range(1, count) if counts[i] < bound]
        whole, budget = sum([portions[i] for i in free]), surplus
        for i in free:
            addition = min(bound - counts[i], max(1, budget * portions[i] // whole), surplus)
            counts[i] = counts[i] + addition
            surplus = surplus - addition
    return np.array(counts)


def scatter_about(key, shape, scale, bound, cuts=(), kind=jnp.bfloat16):
    drawn = scale * jax.random.normal(key, shape, jnp.float32)
    if cuts:
        drawn = drawn * steps_of(key, shape, cuts, -0.22, 0.18)
    return jnp.clip(drawn, -bound, bound).astype(kind)


def setup_inputs(seed: int = 0) -> dict:
    streams_of = jax.random.split(jax.random.key(seed), 7)
    visibilities = scatter_about(streams_of[0], (SLOTS, 2, TIMES * CHANS), 1.0, 6.0, ((0, 256),), jnp.float32)
    coords = jnp.clip(jax.random.uniform(streams_of[1], (SLOTS, 2, TIMES), jnp.float32, -11.2, 11.2) * steps_of(streams_of[1], (SLOTS, 2, TIMES), ((0, 256),), -0.4, 0.0), -11.2, 11.2)
    chan_scale = jnp.clip(jax.random.uniform(streams_of[2], (CHANS,), jnp.float32, 0.9, 1.1), 0.9, 1.1)
    taper_gain = jnp.clip(jnp.exp(jax.random.uniform(streams_of[3], (TILE, TILE), jnp.float32, math.log(0.25), math.log(1.0))), 0.25, 1.0)
    owner_base_keys = jax.random.split(jax.random.fold_in(streams_of[4], 1), SLOTS // SLOT_DEV)
    owner_base_turns = jax.random.permutation(jax.random.fold_in(streams_of[4], 3), SLOTS // SLOT_DEV)
    owner_base = jax.vmap(lambda own, number: deal_out(jax.random.fold_in(streams_of[4], 2), own, number, SLOT_DEV, N_BASE, 1, CAP, 2))(owner_base_keys, owner_base_turns).reshape((SLOTS, 1))
    tile_cell = set_ends(jax.random.randint(streams_of[5], (SLOTS,), 0, TPR * TPC), jax.random.fold_in(streams_of[5], 1), 0, (TPR * TPC) - 1).astype(jnp.int32)
    return dict(visibilities=visibilities, coords=coords, chan_scale=chan_scale, taper_gain=taper_gain, owner_base=owner_base, tile_cell=tile_cell)


two_pi = 2.0 * math.pi
exact = lax.Precision.HIGHEST

def phase_table(length, direction):
    indices = jnp.arange(length, dtype=jnp.int32)
    product = indices[:, None] * indices[None, :] % length
    angle = direction * two_pi / length * product.astype(jnp.float32)
    return (jnp.cos(angle), jnp.sin(angle))

def grid_block(samples, places, chan_scale, taper_gain):
    number = samples.shape[0]
    extent = taper_gain.shape[0]
    time_count = places.shape[2]
    sample_count = time_count * chan_scale.shape[0]
    offsets = (jnp.arange(extent, dtype=jnp.float32) - extent // 2) / extent
    u_pos = (places[:, 0, :, None] * chan_scale[None, None, :]).reshape(number, sample_count)
    v_pos = (places[:, 1, :, None] * chan_scale[None, None, :]).reshape(number, sample_count)
    angle_y = two_pi * offsets[None, :, None] * v_pos[:, None, :]
    angle_x = two_pi * offsets[None, :, None] * u_pos[:, None, :]
    cos_y = jnp.cos(angle_y)
    sin_y = jnp.sin(angle_y)
    cos_x = jnp.cos(angle_x)
    sin_x = jnp.sin(angle_x)
    real_in = samples[:, 0:1, :]
    imag_in = samples[:, 1:2, :]
    left_re = real_in * cos_y - imag_in * sin_y
    left_im = real_in * sin_y + imag_in * cos_y

    def pairwise(first_arr, second_arr):
        return jnp.einsum('nyv,nxv->nyx', first_arr, second_arr, precision=exact)
    pix_re = (pairwise(left_re, cos_x) - pairwise(left_im, sin_x)) * taper_gain
    pix_im = (pairwise(left_re, sin_x) + pairwise(left_im, cos_x)) * taper_gain
    f_cos, f_sin = phase_table(extent, 1.0)

    def along_x(values, table):
        return jnp.einsum('nyx,xk->nyk', values, table, precision=exact)

    def along_y(values, table):
        return jnp.einsum('yk,nyx->nkx', table, values, precision=exact)
    q_re = along_x(pix_re, f_cos) + along_x(pix_im, f_sin)
    q_im = along_x(pix_im, f_cos) - along_x(pix_re, f_sin)
    t_re = along_y(q_re, f_cos) + along_y(q_im, f_sin)
    t_im = along_y(q_im, f_cos) - along_y(q_re, f_sin)
    factor = 1.0 / (extent * math.sqrt(sample_count))
    return jnp.stack([t_re, t_im], axis=1).reshape(number, 2, extent * extent) * factor

def make_tiles(samples, places, chan_scale, taper_gain):
    number = samples.shape[0]
    block_size = math.gcd(number, 64)
    blocks = number // block_size

    def one_block(pieces):
        return grid_block(pieces[0], pieces[1], chan_scale, taper_gain)
    result = lax.map(one_block, (samples.reshape(blocks, block_size, 2, samples.shape[2]), places.reshape(blocks, block_size, 2, places.shape[2])))
    return result.reshape(number, 2, result.shape[3])

def reference(visibilities, coords, chan_scale, taper_gain, owner_base, tile_cell):
    row_tiles = G // (TILE * N_BAND)
    col_tiles = G // (TILE * N_BASE)
    cell_span = jnp.arange(TILE, dtype=jnp.int32)
    owners = owner_base[:, 0]

    def step(uv_grid, device_id):
        offset_at = (device_id * SLOT_DEV).astype(jnp.int32)
        samples = lax.dynamic_slice_in_dim(visibilities, offset_at, SLOT_DEV, 0)
        places = lax.dynamic_slice_in_dim(coords, offset_at, SLOT_DEV, 0)
        own_ids = lax.dynamic_slice_in_dim(owners, offset_at, SLOT_DEV, 0)
        cell_ids = lax.dynamic_slice_in_dim(tile_cell, offset_at, SLOT_DEV, 0)
        tiles = make_tiles(samples, places, chan_scale, taper_gain).reshape(SLOT_DEV, 2, TILE, TILE)
        band_id = device_id % N_BAND
        row_start = (band_id * row_tiles + cell_ids // col_tiles) * TILE
        col_start = (own_ids * col_tiles + cell_ids % col_tiles) * TILE
        row_ids = row_start[:, None, None] + cell_span[None, :, None]
        col_ids = col_start[:, None, None] + cell_span[None, None, :]
        uv_grid = uv_grid.at[0, row_ids, col_ids].add(tiles[:, 0])
        uv_grid = uv_grid.at[1, row_ids, col_ids].add(tiles[:, 1])
        return (uv_grid, None)
    uv_grid, unused = lax.scan(step, jnp.zeros((2, G, G), jnp.float32), jnp.arange(DEVICES, dtype=jnp.int32))
    image = jnp.fft.ifft2(lax.complex(uv_grid[0], uv_grid[1])) * G
    return jnp.stack([jnp.real(image).T, jnp.imag(image).T]).astype(jnp.float32)
```

```python
import functools
import math

import jax
import jax.numpy as jnp
import ml_dtypes
import numpy as np
from jax import lax
from jax.experimental import pallas as pl
from jax.experimental.pallas import tpu as pltpu
from jax.sharding import PartitionSpec as P

G = 8192
TILE = 32
SLOT = 256
PAIRS = SLOT // 2
N_BASE = 32
N_BAND = 8
K_TILES = G // TILE
ROWS = PAIRS + 8
F32 = jnp.float32
BF16 = jnp.bfloat16


def split_np(table):
    table = np.asarray(table, np.float64)
    high = table.astype(np.float32).astype(ml_dtypes.bfloat16)
    low = (table - high.astype(np.float64)).astype(np.float32).astype(ml_dtypes.bfloat16)
    return high, low


def waves(first, second, length):
    turns = np.outer(np.asarray(first), np.asarray(second)) % length
    angle = 2.0 * np.pi / length * turns
    return np.cos(angle), np.sin(angle)


def split(x):
    high = x.astype(BF16)
    low = (x - high.astype(F32)).astype(BF16)
    return high, low


def mm(a, b):
    return lax.dot_general(a, b, (((1,), (0,)), ((), ())), preferred_element_type=F32)


def mm_nt(a, b):
    return lax.dot_general(a, b, (((1,), (1,)), ((), ())), preferred_element_type=F32)


def mm3(ah, al, bh, bl):
    return mm(ah, bh) + (mm(al, bh) + mm(ah, bl))


def fit_waves():
    r = 0.5 * np.cos(np.pi * (np.arange(4000) + 0.5) / 4000)
    odd = np.stack([r ** (2 * i + 1) for i in range(7)], 1)
    even = np.stack([r ** (2 * i) for i in range(8)], 1)
    s = np.linalg.lstsq(odd, np.sin(2 * np.pi * r), rcond=None)[0]
    c = np.linalg.lstsq(even, np.cos(2 * np.pi * r), rcond=None)[0]
    return [float(np.float32(v)) for v in s], [float(np.float32(v)) for v in c]


SIN_C, COS_C = fit_waves()


def cos_sin_turns(turns):
    r = turns - jnp.floor(turns + 0.5)
    r2 = r * r
    s = jnp.full_like(r, SIN_C[-1])
    for v in SIN_C[-2::-1]:
        s = s * r2 + v
    c = jnp.full_like(r, COS_C[-1])
    for v in COS_C[-2::-1]:
        c = c * r2 + v
    return c, s * r


UNIT = 8


def powers(base, w8, w16):
    c, s = base
    c8, s8 = w8
    c16, s16 = w16
    return [
        (c * c16 + s * s16, s * c16 - c * s16),
        (c * c8 + s * s8, s * c8 - c * s8),
        (c, s),
        (c * c8 - s * s8, s * c8 + c * s8),
    ]


def grid_kernel(vr_ref, vi_ref, tu_ref, tv_ref, ids_ref, taper_ref, kxh_ref, kxl_ref, fyh_ref, fyl_ref, out_ref, w_ref):
    step8 = lax.broadcasted_iota(jnp.int32, (8, 128), 0).astype(F32)
    lane = lax.broadcasted_iota(jnp.int32, (32, 128), 1)
    for i, ref in enumerate((tu_ref, tv_ref)):
        for j in range(0, SLOT, 64):
            rows = pl.ds(j, 64)
            c8, s8 = cos_sin_turns(ref[rows, :] * 8.0)
            w_ref[4 * i, rows, :] = c8
            w_ref[4 * i + 1, rows, :] = s8
            w_ref[4 * i + 2, rows, :] = c8 * c8 - s8 * s8
            w_ref[4 * i + 3, rows, :] = 2.0 * (c8 * s8)
    pad = jnp.zeros((8, 128), F32)
    ids_pad = jnp.where(lax.broadcasted_iota(jnp.int32, (8, 128), 0) < 2, ids_ref[...], pad)
    for k in range(TILE):
        out_ref[pl.ds(k * ROWS + PAIRS, 8), :] = ids_pad

    def one(s):
        row = pl.ds(s, 1)

        def phases(ref, first):
            turns = ref[row, :] * step8
            w = [jnp.broadcast_to(w_ref[first + i, row, :], (8, 128)) for i in range(4)]
            return powers(cos_sin_turns(turns), (w[0], w[1]), (w[2], w[3]))

        x_side = phases(tu_ref, 0)
        y_side = phases(tv_ref, 4)
        vr = jnp.broadcast_to(vr_ref[row, :], (8, 128))
        vi = jnp.broadcast_to(vi_ref[row, :], (8, 128))
        l_re = jnp.concatenate([vr * c - vi * s for c, s in y_side], 0)
        l_im = jnp.concatenate([vr * s + vi * c for c, s in y_side], 0)
        c_x = jnp.concatenate([c for c, s in x_side], 0)
        s_x = jnp.concatenate([s for c, s in x_side], 0)
        lrh, lrl = split(l_re)
        lih, lil = split(l_im)
        ch, cl = split(c_x)
        sh, sl = split(s_x)
        left = jnp.concatenate([jnp.concatenate([lrh, lih], 1), jnp.concatenate([lrl, lil], 1)], 0)
        right_h = jnp.concatenate([jnp.concatenate([ch, -sh], 1), jnp.concatenate([sh, ch], 1)], 0)
        right_l = jnp.concatenate([jnp.concatenate([cl, -sl], 1), jnp.concatenate([sl, cl], 1)], 0)
        return left, right_h, right_l

    def body(step, carry):
        first = step * UNIT
        pixels = []
        for pair in range(UNIT // 2):
            a, b = one(first + 2 * pair), one(first + 2 * pair + 1)
            left_h = jnp.concatenate([a[0][0:32], b[0][0:32]], 0)
            left_l = jnp.concatenate([a[0][32:64], b[0][32:64]], 0)
            right_h = jnp.concatenate([a[1], b[1]], 0)
            right_l = jnp.concatenate([a[2], b[2]], 0)
            prod = mm_nt(left_h, right_h) + (mm_nt(left_l, right_h) + mm_nt(left_h, right_l))
            pixels.append(jnp.where(lane < 64, prod[0:32], prod[32:64]) * taper_ref[...])
        ph, pl_ = split(jnp.concatenate(pixels, 0))
        q = mm3(ph, pl_, kxh_ref[...], kxl_ref[...])
        for pair in range(UNIT // 2):
            rows = slice(pair * 32, pair * 32 + 32)
            col = jnp.concatenate([q[rows, 0:128], q[rows, 128:256]], 0)
            qh, ql = split(col)
            tile = mm(fyh_ref[...], qh) + (mm(fyl_ref[...], qh) + mm(fyh_ref[...], ql))
            out_ref[pl.ds(step * (UNIT // 2) + pair, 32, stride=ROWS), :] = tile
        return carry

    lax.fori_loop(0, SLOT // UNIT, body, 0)


def grid_tables():
    span = np.arange(TILE)
    c, s = waves(span, span, TILE)
    eye2 = np.eye(2)
    fx = np.block([[c, -s], [s, c]])
    fx_turned = np.block([[-s, -c], [c, -s]])
    kx = np.concatenate([np.kron(eye2, fx), np.kron(eye2, fx_turned)], 1)
    fy = np.concatenate([c, s], 1) / (TILE * math.sqrt(128.0))
    return split_np(kx) + split_np(fy)


def row_kernel(ids_ref, in_ref, eh_ref, el_ref, tc_ref, ts_ref, fh_ref, fl_ref, out_ref, acc_a, acc_b, z_ref):
    def clear(i, carry):
        rows = pl.ds(pl.multiple_of(i * 64, 64), 64)
        acc_a[rows, :] = jnp.zeros((64, 128), F32)
        acc_b[rows, :] = jnp.zeros((64, 128), F32)
        return carry

    lax.fori_loop(0, G // 64, clear, 0)

    def add(i, carry):
        src = i // (PAIRS // 8)
        block = i % (PAIRS // 8)
        base = src * SLOT + block * 8
        rows = in_ref[src, pl.ds(pl.multiple_of(block * 8, 8), 8), :]
        for t in range(8):
            at_a = pl.ds(ids_ref[base + t], 1)
            at_b = pl.ds(ids_ref[base + PAIRS + t], 1)
            acc_a[at_a, :] = acc_a[at_a, :] + rows[t : t + 1]
            acc_b[at_b, :] = acc_b[at_b, :] + rows[t : t + 1]
        return carry

    lax.fori_loop(0, N_BASE * PAIRS // 8, add, 0)

    low_half = lax.broadcasted_iota(jnp.int32, (K_TILES, 128), 1) < 64

    def rows_of(pair, carry):
        one = pl.ds(pl.multiple_of(pair * (2 * K_TILES), K_TILES), K_TILES)
        two = pl.ds(pl.multiple_of(pair * (2 * K_TILES) + K_TILES, K_TILES), K_TILES)
        a1, a2 = acc_a[one, :], acc_a[two, :]
        b1, b2 = acc_b[one, :], acc_b[two, :]
        held = jnp.where(low_half, a1, b2) + pltpu.roll(jnp.where(low_half, a2, b1), 64, 1)
        hh, hl = split(held.T)
        prod = mm3(hh, hl, eh_ref[...], el_ref[...])
        parts = []
        for t in range(2):
            re, im = prod[64 * t : 64 * t + 32], prod[64 * t + 32 : 64 * t + 64]
            y_re = re[:, 0:256] - im[:, 256:512]
            y_im = re[:, 256:512] + im[:, 0:256]
            parts.append(y_re * tc_ref[...] - y_im * ts_ref[...])
            parts.append(y_re * ts_ref[...] + y_im * tc_ref[...])
        vh, vl = split(jnp.concatenate(parts, 0))
        z = mm3(fh_ref[...], fl_ref[...], vh, vl)
        for half in range(2):
            z_ref[half, pl.ds(pl.multiple_of(pair * 128, 128), 128), :] = z[:, 128 * half : 128 * half + 128]
        return carry

    lax.fori_loop(0, TILE // 2, rows_of, 0)

    quarter = lax.broadcasted_iota(jnp.int32, (16, 128), 1) // 32

    def send(b2, carry):
        for half in range(2):
            parts = [z_ref[half, pl.ds(c * 32 + b2, 32, stride=64), :] for c in range(2)]
            pieces = [parts[c][16 * r : 16 * r + 16] for r in range(2) for c in range(2)]
            for zq in range(4):
                block = None
                for p in range(4):
                    moved = pieces[p] if p == zq else pltpu.roll(pieces[p], (p - zq) * 32 % 128, 1)
                    block = moved if block is None else jnp.where(quarter == p, moved, block)
                out_ref[b2 * N_BAND + half * 4 + zq] = block
        return carry

    lax.fori_loop(0, N_BASE, send, 0)


def row_tables():
    span = np.arange(K_TILES)
    c, s = waves(span, span, K_TILES)
    e = np.concatenate([c, s], 1)
    kx = np.arange(TILE)
    tc, ts = waves(kx, span, G)
    c32, s32 = waves(kx, kx, TILE)
    f = np.kron(np.eye(2), np.block([[c32, -s32], [s32, c32]]))
    return split_np(e) + (tc.astype(np.float32), ts.astype(np.float32)) + split_np(f)


def column_kernel(in_ref, eh_ref, el_ref, tc_ref, ts_ref, fh_ref, fl_ref, out_ref, v_ref, x_ref):
    def first(group, carry):
        lefts = []
        for t in range(4):
            block = in_ref[pl.ds((group * 4 + t) * N_BAND, N_BAND)].reshape(128, 128)
            turned = block.T
            lefts.append(jnp.concatenate([turned[0:64], turned[64:128]], 1))
        dh, dl = split(jnp.concatenate(lefts, 0))
        prod = mm3(dh, dl, eh_ref[...], el_ref[...])
        for t in range(4):
            j = group * 4 + t
            re, im = prod[64 * t : 64 * t + 32], prod[64 * t + 32 : 64 * t + 64]
            y_re = re[:, 0:256] - im[:, 256:512]
            y_im = re[:, 256:512] + im[:, 0:256]
            tc = tc_ref[pl.ds(j, 1), :]
            ts = ts_ref[pl.ds(j, 1), :]
            v_re = y_re * tc - y_im * ts
            v_im = y_re * ts + y_im * tc
            for half in range(2):
                lanes = slice(128 * half, 128 * half + 128)
                v_ref[half, pl.ds(j, 32, stride=64), :] = v_re[:, lanes]
                v_ref[half, pl.ds(32 + j, 32, stride=64), :] = v_im[:, lanes]
        return carry

    lax.fori_loop(0, N_BASE // 4, first, 0)

    def second(b, carry):
        rows = pl.ds(pl.multiple_of(b * 64, 64), 64)
        vh, vl = split(jnp.concatenate([v_ref[0, rows, :], v_ref[1, rows, :]], 1))
        x = mm3(fh_ref[...], fl_ref[...], vh, vl)
        for half in range(2):
            x_ref[half, rows, :] = x[:, 128 * half : 128 * half + 128]
        return carry

    lax.fori_loop(0, TILE, second, 0)
    for c in range(2):
        for a2 in range(TILE):
            for half in range(2):
                at = a2 * 256 + half * 128
                out_ref[c, :, at : at + 128] = x_ref[half, pl.ds(c * 32 + a2, 32, stride=64), :]


def column_tables():
    zs, rp, rpp = np.arange(8), np.arange(16), np.arange(2)
    r = (rpp[:, None, None] * 16 + zs[None, :, None] * 32 + rp[None, None, :]).reshape(-1)
    span = np.arange(K_TILES)
    c, s = waves(r, span, K_TILES)
    e = np.concatenate([c, s], 1)
    ky = np.arange(TILE)
    tc, ts = waves(ky, span, G)
    c32, s32 = waves(ky, ky, TILE)
    f = np.block([[c32, -s32], [s32, c32]]) / G
    return split_np(e) + (tc.astype(np.float32), ts.astype(np.float32)) + split_np(f)


VMEM = pl.BlockSpec(memory_space=pltpu.VMEM)
SMEM = pl.BlockSpec(memory_space=pltpu.SMEM)
LIMIT = pltpu.CompilerParams(vmem_limit_bytes=56 * 2**20)


def shards(visibilities, coords, chan_scale, taper_gain, owner_base, tile_cell):
    places = (coords[:, :, :, None] * chan_scale).reshape(SLOT, 2, 128) * (1.0 / TILE)
    ids = (tile_cell // 8) * K_TILES + owner_base[:, 0] * 8 + tile_cell % 8
    ids = ids.reshape(PAIRS, 2).T.astype(F32)
    ids = jnp.concatenate([ids, jnp.zeros((6, PAIRS), F32)], 0)
    taper = jnp.tile(taper_gain, (1, 4))
    sent = pl.pallas_call(
        grid_kernel,
        out_shape=jax.ShapeDtypeStruct((TILE * ROWS, 128), F32),
        in_specs=[VMEM] * 10,
        out_specs=VMEM,
        scratch_shapes=[pltpu.VMEM((8, SLOT, 128), F32)],
        compiler_params=LIMIT,
        name="gridding",
    )(
        visibilities[:, 0, :],
        visibilities[:, 1, :],
        places[:, 0, :],
        places[:, 1, :],
        ids,
        taper,
        *[jnp.asarray(t) for t in grid_tables()],
    )
    arrived = lax.all_to_all(sent.reshape(N_BASE, ROWS, 128), "base", split_axis=0, concat_axis=0, tiled=True)
    where = arrived[:, PAIRS : PAIRS + 2, :].astype(jnp.int32).reshape(N_BASE * SLOT)
    rows = pl.pallas_call(
        row_kernel,
        out_shape=jax.ShapeDtypeStruct((N_BASE * N_BAND, 16, 128), F32),
        in_specs=[SMEM] + [VMEM] * 7,
        out_specs=VMEM,
        scratch_shapes=[
            pltpu.VMEM((G, 128), F32),
            pltpu.VMEM((G, 128), F32),
            pltpu.VMEM((2, TILE * 64, 128), F32),
        ],
        compiler_params=LIMIT,
        name="rows",
    )(where, arrived, *[jnp.asarray(t) for t in row_tables()])
    turned = lax.all_to_all(rows, ("base", "band"), split_axis=0, concat_axis=0, tiled=True)
    return pl.pallas_call(
        column_kernel,
        out_shape=jax.ShapeDtypeStruct((2, TILE, G), F32),
        in_specs=[VMEM] * 7,
        out_specs=VMEM,
        scratch_shapes=[pltpu.VMEM((2, TILE * 64, 128), F32), pltpu.VMEM((2, TILE * 64, 128), F32)],
        compiler_params=LIMIT,
        name="columns",
    )(turned, *[jnp.asarray(t) for t in column_tables()])


def solution(mesh):
    placed = (
        P(("base", "band"), None, None),
        P(("base", "band"), None, None),
        P(),
        P(),
        P(("base", "band"), None),
        P(("base", "band")),
    )
    return jax.shard_map(
        shards,
        mesh=mesh,
        in_specs=placed,
        out_specs=P(None, ("base", "band"), None),
        check_vma=False,
    )
```

```python
import functools
import math

import jax
import jax.numpy as jnp
import ml_dtypes
import numpy as np
from jax import lax
from jax.experimental import pallas as pl
from jax.experimental.pallas import tpu as pltpu
from jax.sharding import PartitionSpec as P

G = 8192
TILE = 32
SLOT = 256
PAIRS = SLOT // 2
N_BASE = 32
N_BAND = 8
K_TILES = G // TILE
ROWS = PAIRS + 8
F32 = jnp.float32
BF16 = jnp.bfloat16


def split_np(table):
    table = np.asarray(table, np.float64)
    high = table.astype(np.float32).astype(ml_dtypes.bfloat16)
    low = (table - high.astype(np.float64)).astype(np.float32).astype(ml_dtypes.bfloat16)
    return high, low


def waves(first, second, length):
    turns = np.outer(np.asarray(first), np.asarray(second)) % length
    angle = 2.0 * np.pi / length * turns
    return np.cos(angle), np.sin(angle)


def split(x):
    high = x.astype(BF16)
    low = (x - high.astype(F32)).astype(BF16)
    return high, low


def mm(a, b):
    return lax.dot_general(a, b, (((1,), (0,)), ((), ())), preferred_element_type=F32)


def mm_nt(a, b):
    return lax.dot_general(a, b, (((1,), (1,)), ((), ())), preferred_element_type=F32)


def mm3(ah, al, bh, bl):
    return mm(ah, bh) + (mm(al, bh) + mm(ah, bl))


def fit_waves():
    r = 0.5 * np.cos(np.pi * (np.arange(4000) + 0.5) / 4000)
    odd = np.stack([r ** (2 * i + 1) for i in range(7)], 1)
    even = np.stack([r ** (2 * i) for i in range(8)], 1)
    s = np.linalg.lstsq(odd, np.sin(2 * np.pi * r), rcond=None)[0]
    c = np.linalg.lstsq(even, np.cos(2 * np.pi * r), rcond=None)[0]
    return [float(np.float32(v)) for v in s], [float(np.float32(v)) for v in c]


SIN_C, COS_C = fit_waves()


def cos_sin_turns(turns):
    r = turns - jnp.floor(turns + 0.5)
    r2 = r * r
    s = jnp.full_like(r, SIN_C[-1])
    for v in SIN_C[-2::-1]:
        s = s * r2 + v
    c = jnp.full_like(r, COS_C[-1])
    for v in COS_C[-2::-1]:
        c = c * r2 + v
    return c, s * r


UNIT = 32
CHAINS = 8
STEP = 64


def powers(base, w8, w16):
    c, s = base
    c8, s8 = w8
    c16, s16 = w16
    return [
        (c * c16 + s * s16, s * c16 - c * s16),
        (c * c8 + s * s8, s * c8 - c * s8),
        (c, s),
        (c * c8 - s * s8, s * c8 + c * s8),
    ]


def grid_kernel(vr_ref, vi_ref, tu_ref, tv_ref, ids_ref, taper_ref, kxh_ref, kxl_ref, fyh_ref, fyl_ref, out_ref, w_ref):
    step8 = lax.broadcasted_iota(jnp.int32, (8, 128), 0).astype(F32)
    lane = lax.broadcasted_iota(jnp.int32, (32, 128), 1)
    for i, ref in enumerate((tu_ref, tv_ref)):
        for j in range(0, SLOT, 64):
            rows = pl.ds(j, 64)
            c8, s8 = cos_sin_turns(ref[rows, :] * 8.0)
            w_ref[4 * i, rows, :] = c8
            w_ref[4 * i + 1, rows, :] = s8
            w_ref[4 * i + 2, rows, :] = c8 * c8 - s8 * s8
            w_ref[4 * i + 3, rows, :] = 2.0 * (c8 * s8)
    pad = jnp.zeros((8, 128), F32)
    ids_pad = jnp.where(lax.broadcasted_iota(jnp.int32, (8, 128), 0) < 2, ids_ref[...], pad)
    for k in range(TILE):
        out_ref[pl.ds(k * ROWS + PAIRS, 8), :] = ids_pad

    def one(s):
        row = pl.ds(s, 1)

        def phases(ref, first):
            turns = ref[row, :] * step8
            w = [jnp.broadcast_to(w_ref[first + i, row, :], (8, 128)) for i in range(4)]
            return powers(cos_sin_turns(turns), (w[0], w[1]), (w[2], w[3]))

        x_side = phases(tu_ref, 0)
        y_side = phases(tv_ref, 4)
        vr = jnp.broadcast_to(vr_ref[row, :], (8, 128))
        vi = jnp.broadcast_to(vi_ref[row, :], (8, 128))
        l_re = jnp.concatenate([vr * c - vi * s for c, s in y_side], 0)
        l_im = jnp.concatenate([vr * s + vi * c for c, s in y_side], 0)
        c_x = jnp.concatenate([c for c, s in x_side], 0)
        s_x = jnp.concatenate([s for c, s in x_side], 0)
        lrh, lrl = split(l_re)
        lih, lil = split(l_im)
        ch, cl = split(c_x)
        sh, sl = split(s_x)
        left = jnp.concatenate([jnp.concatenate([lrh, lih], 1), jnp.concatenate([lrl, lil], 1)], 0)
        right_h = jnp.concatenate([jnp.concatenate([ch, -sh], 1), jnp.concatenate([sh, ch], 1)], 0)
        right_l = jnp.concatenate([jnp.concatenate([cl, -sl], 1), jnp.concatenate([sl, cl], 1)], 0)
        return left, right_h, right_l

    def body(step, carry):
        first = step * UNIT
        pixels = []
        for pair in range(UNIT // 2):
            a, b = one(first + 2 * pair), one(first + 2 * pair + 1)
            left_h = jnp.concatenate([a[0][0:32], b[0][0:32]], 0)
            left_l = jnp.concatenate([a[0][32:64], b[0][32:64]], 0)
            right_h = jnp.concatenate([a[1], b[1]], 0)
            right_l = jnp.concatenate([a[2], b[2]], 0)
            prod = mm_nt(left_h, right_h) + (mm_nt(left_l, right_h) + mm_nt(left_h, right_l))
            pixels.append(jnp.where(lane < 64, prod[0:32], prod[32:64]) * taper_ref[...])
        ph, pl_ = split(jnp.concatenate(pixels, 0))
        q = mm3(ph, pl_, kxh_ref[...], kxl_ref[...])
        for pair in range(UNIT // 2):
            rows = slice(pair * 32, pair * 32 + 32)
            col = jnp.concatenate([q[rows, 0:128], q[rows, 128:256]], 0)
            qh, ql = split(col)
            tile = mm(fyh_ref[...], qh) + (mm(fyl_ref[...], qh) + mm(fyh_ref[...], ql))
            out_ref[pl.ds(step * (UNIT // 2) + pair, 32, stride=ROWS), :] = tile
        return carry

    lax.fori_loop(0, SLOT // UNIT, body, 0)


def grid_tables():
    span = np.arange(TILE)
    c, s = waves(span, span, TILE)
    eye2 = np.eye(2)
    fx = np.block([[c, -s], [s, c]])
    fx_turned = np.block([[-s, -c], [c, -s]])
    kx = np.concatenate([np.kron(eye2, fx), np.kron(eye2, fx_turned)], 1)
    fy = np.concatenate([c, s], 1) / (TILE * math.sqrt(128.0))
    return split_np(kx) + split_np(fy)


def row_kernel(ids_ref, in_ref, eh_ref, el_ref, tc_ref, ts_ref, fh_ref, fl_ref, out_ref, z_ref, *accs):
    def clear(i, carry):
        rows = pl.ds(pl.multiple_of(i * 64, 64), 64)
        for acc in accs:
            acc[rows, :] = jnp.zeros((64, 128), F32)
        return carry

    lax.fori_loop(0, G // 64, clear, 0)

    def add(i, carry):
        src = i // (PAIRS // STEP)
        block = i % (PAIRS // STEP)
        base = src * SLOT + block * STEP
        rows = in_ref[src, pl.ds(pl.multiple_of(block * STEP, STEP), STEP), :]
        for t in range(STEP):
            for half in range(2):
                acc = accs[(2 * t + half) % CHAINS]
                at = pl.ds(ids_ref[base + half * PAIRS + t], 1)
                acc[at, :] = acc[at, :] + rows[t : t + 1]
        return carry

    lax.fori_loop(0, N_BASE * PAIRS // STEP, add, 0)

    def total(half, rows):
        parts = [acc[rows, :] for acc in accs[half::2]]
        while len(parts) > 1:
            parts = [x + y for x, y in zip(parts[::2], parts[1::2])]
        return parts[0]

    low_half = lax.broadcasted_iota(jnp.int32, (K_TILES, 128), 1) < 64

    def rows_of(pair, carry):
        one = pl.ds(pl.multiple_of(pair * (2 * K_TILES), K_TILES), K_TILES)
        two = pl.ds(pl.multiple_of(pair * (2 * K_TILES) + K_TILES, K_TILES), K_TILES)
        a1, a2 = total(0, one), total(0, two)
        b1, b2 = total(1, one), total(1, two)
        held = jnp.where(low_half, a1, b2) + pltpu.roll(jnp.where(low_half, a2, b1), 64, 1)
        hh, hl = split(held.T)
        prod = mm3(hh, hl, eh_ref[...], el_ref[...])
        parts = []
        for t in range(2):
            re, im = prod[64 * t : 64 * t + 32], prod[64 * t + 32 : 64 * t + 64]
            y_re = re[:, 0:256] - im[:, 256:512]
            y_im = re[:, 256:512] + im[:, 0:256]
            parts.append(y_re * tc_ref[...] - y_im * ts_ref[...])
            parts.append(y_re * ts_ref[...] + y_im * tc_ref[...])
        vh, vl = split(jnp.concatenate(parts, 0))
        z = mm3(fh_ref[...], fl_ref[...], vh, vl)
        for half in range(2):
            z_ref[half, pl.ds(pl.multiple_of(pair * 128, 128), 128), :] = z[:, 128 * half : 128 * half + 128]
        return carry

    lax.fori_loop(0, TILE // 2, rows_of, 0, unroll=4)

    quarter = lax.broadcasted_iota(jnp.int32, (16, 128), 1) // 32

    def send(b2, carry):
        for half in range(2):
            parts = [z_ref[half, pl.ds(c * 32 + b2, 32, stride=64), :] for c in range(2)]
            pieces = [parts[c][16 * r : 16 * r + 16] for r in range(2) for c in range(2)]
            for zq in range(4):
                block = None
                for p in range(4):
                    moved = pieces[p] if p == zq else pltpu.roll(pieces[p], (p - zq) * 32 % 128, 1)
                    block = moved if block is None else jnp.where(quarter == p, moved, block)
                out_ref[b2 * N_BAND + half * 4 + zq] = block
        return carry

    lax.fori_loop(0, N_BASE, send, 0, unroll=4)


def row_tables():
    span = np.arange(K_TILES)
    c, s = waves(span, span, K_TILES)
    e = np.concatenate([c, s], 1)
    kx = np.arange(TILE)
    tc, ts = waves(kx, span, G)
    c32, s32 = waves(kx, kx, TILE)
    f = np.kron(np.eye(2), np.block([[c32, -s32], [s32, c32]]))
    return split_np(e) + (tc.astype(np.float32), ts.astype(np.float32)) + split_np(f)


def column_kernel(in_ref, eh_ref, el_ref, tc_ref, ts_ref, fh_ref, fl_ref, out_ref, v_ref, x_ref):
    def first(group, carry):
        lefts = []
        for t in range(4):
            block = in_ref[pl.ds((group * 4 + t) * N_BAND, N_BAND)].reshape(128, 128)
            turned = block.T
            lefts.append(jnp.concatenate([turned[0:64], turned[64:128]], 1))
        dh, dl = split(jnp.concatenate(lefts, 0))
        prod = mm3(dh, dl, eh_ref[...], el_ref[...])
        for t in range(4):
            j = group * 4 + t
            re, im = prod[64 * t : 64 * t + 32], prod[64 * t + 32 : 64 * t + 64]
            y_re = re[:, 0:256] - im[:, 256:512]
            y_im = re[:, 256:512] + im[:, 0:256]
            tc = tc_ref[pl.ds(j, 1), :]
            ts = ts_ref[pl.ds(j, 1), :]
            v_re = y_re * tc - y_im * ts
            v_im = y_re * ts + y_im * tc
            for half in range(2):
                lanes = slice(128 * half, 128 * half + 128)
                v_ref[half, pl.ds(j, 32, stride=64), :] = v_re[:, lanes]
                v_ref[half, pl.ds(32 + j, 32, stride=64), :] = v_im[:, lanes]
        return carry

    lax.fori_loop(0, N_BASE // 4, first, 0, unroll=8)

    def second(b, carry):
        rows = pl.ds(pl.multiple_of(b * 64, 64), 64)
        vh, vl = split(jnp.concatenate([v_ref[0, rows, :], v_ref[1, rows, :]], 1))
        x = mm3(fh_ref[...], fl_ref[...], vh, vl)
        for half in range(2):
            x_ref[half, rows, :] = x[:, 128 * half : 128 * half + 128]
        return carry

    lax.fori_loop(0, TILE, second, 0, unroll=16)
    for c in range(2):
        for a2 in range(TILE):
            for half in range(2):
                at = a2 * 256 + half * 128
                out_ref[c, :, at : at + 128] = x_ref[half, pl.ds(c * 32 + a2, 32, stride=64), :]


def column_tables():
    zs, rp, rpp = np.arange(8), np.arange(16), np.arange(2)
    r = (rpp[:, None, None] * 16 + zs[None, :, None] * 32 + rp[None, None, :]).reshape(-1)
    span = np.arange(K_TILES)
    c, s = waves(r, span, K_TILES)
    e = np.concatenate([c, s], 1)
    ky = np.arange(TILE)
    tc, ts = waves(ky, span, G)
    c32, s32 = waves(ky, ky, TILE)
    f = np.block([[c32, -s32], [s32, c32]]) / G
    return split_np(e) + (tc.astype(np.float32), ts.astype(np.float32)) + split_np(f)


VMEM = pl.BlockSpec(memory_space=pltpu.VMEM)
SMEM = pl.BlockSpec(memory_space=pltpu.SMEM)
LIMIT = pltpu.CompilerParams(vmem_limit_bytes=56 * 2**20)


def shards(visibilities, coords, chan_scale, taper_gain, owner_base, tile_cell):
    places = (coords[:, :, :, None] * chan_scale).reshape(SLOT, 2, 128) * (1.0 / TILE)
    ids = (tile_cell // 8) * K_TILES + owner_base[:, 0] * 8 + tile_cell % 8
    ids = ids.reshape(PAIRS, 2).T.astype(F32)
    ids = jnp.concatenate([ids, jnp.zeros((6, PAIRS), F32)], 0)
    taper = jnp.tile(taper_gain, (1, 4))
    sent = pl.pallas_call(
        grid_kernel,
        out_shape=jax.ShapeDtypeStruct((TILE * ROWS, 128), F32),
        in_specs=[VMEM] * 10,
        out_specs=VMEM,
        scratch_shapes=[pltpu.VMEM((8, SLOT, 128), F32)],
        compiler_params=LIMIT,
        name="gridding",
    )(
        visibilities[:, 0, :],
        visibilities[:, 1, :],
        places[:, 0, :],
        places[:, 1, :],
        ids,
        taper,
        *[jnp.asarray(t) for t in grid_tables()],
    )
    arrived = lax.all_to_all(sent.reshape(N_BASE, ROWS, 128), "base", split_axis=0, concat_axis=0, tiled=True)
    where = arrived[:, PAIRS : PAIRS + 2, :].astype(jnp.int32).reshape(N_BASE * SLOT)
    rows = pl.pallas_call(
        row_kernel,
        out_shape=jax.ShapeDtypeStruct((N_BASE * N_BAND, 16, 128), F32),
        in_specs=[SMEM] + [VMEM] * 7,
        out_specs=VMEM,
        scratch_shapes=[
            pltpu.VMEM((2, TILE * 64, 128), F32),
            *[pltpu.VMEM((G, 128), F32)] * CHAINS,
        ],
        compiler_params=LIMIT,
        name="rows",
    )(where, arrived, *[jnp.asarray(t) for t in row_tables()])
    turned = lax.all_to_all(rows, ("base", "band"), split_axis=0, concat_axis=0, tiled=True)
    return pl.pallas_call(
        column_kernel,
        out_shape=jax.ShapeDtypeStruct((2, TILE, G), F32),
        in_specs=[VMEM] * 7,
        out_specs=VMEM,
        scratch_shapes=[pltpu.VMEM((2, TILE * 64, 128), F32), pltpu.VMEM((2, TILE * 64, 128), F32)],
        compiler_params=LIMIT,
        name="columns",
    )(turned, *[jnp.asarray(t) for t in column_tables()])


def solution(mesh):
    placed = (
        P(("base", "band"), None, None),
        P(("base", "band"), None, None),
        P(),
        P(),
        P(("base", "band"), None),
        P(("base", "band")),
    )
    return jax.shard_map(
        shards,
        mesh=mesh,
        in_specs=placed,
        out_specs=P(None, ("base", "band"), None),
        check_vma=False,
    )
```

```python
import functools
import math

import jax
import jax.numpy as jnp
import ml_dtypes
import numpy as np
from jax import lax
from jax.experimental import pallas as pl
from jax.experimental.pallas import tpu as pltpu
from jax.sharding import PartitionSpec as P

G = 8192
TILE = 32
SLOT = 256
PAIRS = SLOT // 2
N_BASE = 32
N_BAND = 8
K_TILES = G // TILE
ROWS = PAIRS + 8
F32 = jnp.float32
BF16 = jnp.bfloat16


def split_np(table):
    table = np.asarray(table, np.float64)
    high = table.astype(np.float32).astype(ml_dtypes.bfloat16)
    low = (table - high.astype(np.float64)).astype(np.float32).astype(ml_dtypes.bfloat16)
    return high, low


def waves(first, second, length):
    turns = np.outer(np.asarray(first), np.asarray(second)) % length
    angle = 2.0 * np.pi / length * turns
    return np.cos(angle), np.sin(angle)


def split(x):
    high = x.astype(BF16)
    low = (x - high.astype(F32)).astype(BF16)
    return high, low


def mm(a, b):
    return lax.dot_general(a, b, (((1,), (0,)), ((), ())), preferred_element_type=F32)


def mm_nt(a, b):
    return lax.dot_general(a, b, (((1,), (1,)), ((), ())), preferred_element_type=F32)


def mm3(ah, al, bh, bl):
    return mm(ah, bh) + (mm(al, bh) + mm(ah, bl))


def fit_waves():
    r = 0.5 * np.cos(np.pi * (np.arange(4000) + 0.5) / 4000)
    odd = np.stack([r ** (2 * i + 1) for i in range(7)], 1)
    even = np.stack([r ** (2 * i) for i in range(8)], 1)
    s = np.linalg.lstsq(odd, np.sin(2 * np.pi * r), rcond=None)[0]
    c = np.linalg.lstsq(even, np.cos(2 * np.pi * r), rcond=None)[0]
    return [float(np.float32(v)) for v in s], [float(np.float32(v)) for v in c]


SIN_C, COS_C = fit_waves()


def cos_sin_turns(turns):
    r = turns - jnp.floor(turns + 0.5)
    r2 = r * r
    s = jnp.full_like(r, SIN_C[-1])
    for v in SIN_C[-2::-1]:
        s = s * r2 + v
    c = jnp.full_like(r, COS_C[-1])
    for v in COS_C[-2::-1]:
        c = c * r2 + v
    return c, s * r


UNIT = 32
SENDS = 4
MESH = pl.DeviceIdType.MESH
OFFSETS = sorted(
    [(x, y, c) for x in range(4) for y in range(4) for c in range(2) if (x, y, c) != (0, 0, 0)],
    key=lambda d: ((d[0] + d[1]) % 4, d[0], d[2]),
)


def moved(base, offset):
    x, y, c = base // 8, base // 2 % 4, base % 2
    return (x + offset[0]) % 4 * 8 + (y + offset[1]) % 4 * 2 + (c + offset[2]) % 2
CHAINS = 8
STEP = 64


def powers(base, w8, w16):
    c, s = base
    c8, s8 = w8
    c16, s16 = w16
    return [
        (c * c16 + s * s16, s * c16 - c * s16),
        (c * c8 + s * s8, s * c8 - c * s8),
        (c, s),
        (c * c8 - s * s8, s * c8 + c * s8),
    ]


def grid_kernel(vr_ref, vi_ref, tu_ref, tv_ref, ids_ref, taper_ref, kxh_ref, kxl_ref, fyh_ref, fyl_ref, all_ref, w_ref, out_ref, send_sem, recv_sem, own_sem):
    base, band = lax.axis_index("base"), lax.axis_index("band")
    barrier = pltpu.get_barrier_semaphore()
    for offset in OFFSETS:
        pl.semaphore_signal(barrier, inc=1, device_id=(moved(base, offset), band), device_id_type=MESH)
    step8 = lax.broadcasted_iota(jnp.int32, (8, 128), 0).astype(F32)
    lane = lax.broadcasted_iota(jnp.int32, (32, 128), 1)
    for i, ref in enumerate((tu_ref, tv_ref)):
        for j in range(0, SLOT, 64):
            rows = pl.ds(j, 64)
            c8, s8 = cos_sin_turns(ref[rows, :] * 8.0)
            w_ref[4 * i, rows, :] = c8
            w_ref[4 * i + 1, rows, :] = s8
            w_ref[4 * i + 2, rows, :] = c8 * c8 - s8 * s8
            w_ref[4 * i + 3, rows, :] = 2.0 * (c8 * s8)
    pad = jnp.zeros((8, 128), F32)
    ids_pad = jnp.where(lax.broadcasted_iota(jnp.int32, (8, 128), 0) < 2, ids_ref[...], pad)
    for k in range(TILE):
        out_ref[pl.ds(k * ROWS + PAIRS, 8), :] = ids_pad

    def one(s):
        row = pl.ds(s, 1)

        def phases(ref, first):
            turns = ref[row, :] * step8
            w = [jnp.broadcast_to(w_ref[first + i, row, :], (8, 128)) for i in range(4)]
            return powers(cos_sin_turns(turns), (w[0], w[1]), (w[2], w[3]))

        x_side = phases(tu_ref, 0)
        y_side = phases(tv_ref, 4)
        vr = jnp.broadcast_to(vr_ref[row, :], (8, 128))
        vi = jnp.broadcast_to(vi_ref[row, :], (8, 128))
        l_re = jnp.concatenate([vr * c - vi * s for c, s in y_side], 0)
        l_im = jnp.concatenate([vr * s + vi * c for c, s in y_side], 0)
        c_x = jnp.concatenate([c for c, s in x_side], 0)
        s_x = jnp.concatenate([s for c, s in x_side], 0)
        lrh, lrl = split(l_re)
        lih, lil = split(l_im)
        ch, cl = split(c_x)
        sh, sl = split(s_x)
        left = jnp.concatenate([jnp.concatenate([lrh, lih], 1), jnp.concatenate([lrl, lil], 1)], 0)
        right_h = jnp.concatenate([jnp.concatenate([ch, -sh], 1), jnp.concatenate([sh, ch], 1)], 0)
        right_l = jnp.concatenate([jnp.concatenate([cl, -sl], 1), jnp.concatenate([sl, cl], 1)], 0)
        return left, right_h, right_l

    def body(step, carry):
        first = step * UNIT
        pixels = []
        for pair in range(UNIT // 2):
            a, b = one(first + 2 * pair), one(first + 2 * pair + 1)
            left_h = jnp.concatenate([a[0][0:32], b[0][0:32]], 0)
            left_l = jnp.concatenate([a[0][32:64], b[0][32:64]], 0)
            right_h = jnp.concatenate([a[1], b[1]], 0)
            right_l = jnp.concatenate([a[2], b[2]], 0)
            prod = mm_nt(left_h, right_h) + (mm_nt(left_l, right_h) + mm_nt(left_h, right_l))
            pixels.append(jnp.where(lane < 64, prod[0:32], prod[32:64]) * taper_ref[...])
        ph, pl_ = split(jnp.concatenate(pixels, 0))
        q = mm3(ph, pl_, kxh_ref[...], kxl_ref[...])
        for pair in range(UNIT // 2):
            rows = slice(pair * 32, pair * 32 + 32)
            col = jnp.concatenate([q[rows, 0:128], q[rows, 128:256]], 0)
            qh, ql = split(col)
            tile = mm(fyh_ref[...], qh) + (mm(fyl_ref[...], qh) + mm(fyh_ref[...], ql))
            out_ref[pl.ds(step * (UNIT // 2) + pair, 32, stride=ROWS), :] = tile
        return carry

    steps = SLOT // UNIT // SENDS

    def send(part, rows):
        for offset in OFFSETS:
            to = moved(base, offset)
            pltpu.make_async_remote_copy(
                src_ref=out_ref.at[pl.ds(pl.multiple_of(to * ROWS + part, 8), rows), :],
                dst_ref=all_ref.at[base, pl.ds(pl.multiple_of(part, 8), rows), :],
                send_sem=send_sem,
                recv_sem=recv_sem,
                device_id=(to, band),
                device_id_type=MESH,
            ).start()

    rows = PAIRS // SENDS
    lax.fori_loop(0, steps, body, 0)
    pl.semaphore_wait(barrier, len(OFFSETS))
    send(0, rows)

    def later(part, carry):
        lax.fori_loop(part * steps, part * steps + steps, body, 0)
        send(part * rows, rows)
        return carry

    lax.fori_loop(1, SENDS - 1, later, 0)
    lax.fori_loop(SLOT // UNIT - steps, SLOT // UNIT, body, 0)
    send(PAIRS - rows, rows + 8)
    own = pltpu.make_async_copy(out_ref.at[pl.ds(pl.multiple_of(base * ROWS, 8), ROWS), :], all_ref.at[base], own_sem)
    own.start()
    own.wait()
    sent = out_ref.at[pl.ds(0, len(OFFSETS) * ROWS), :]
    pltpu.make_async_copy(sent, sent, send_sem).wait()
    arrived = all_ref.at[pl.ds(0, len(OFFSETS))]
    pltpu.make_async_copy(arrived, arrived, recv_sem).wait()


def grid_tables():
    span = np.arange(TILE)
    c, s = waves(span, span, TILE)
    eye2 = np.eye(2)
    fx = np.block([[c, -s], [s, c]])
    fx_turned = np.block([[-s, -c], [c, -s]])
    kx = np.concatenate([np.kron(eye2, fx), np.kron(eye2, fx_turned)], 1)
    fy = np.concatenate([c, s], 1) / (TILE * math.sqrt(128.0))
    return split_np(kx) + split_np(fy)


def row_kernel(ids_ref, in_ref, eh_ref, el_ref, tc_ref, ts_ref, fh_ref, fl_ref, out_ref, z_ref, *accs):
    def clear(i, carry):
        rows = pl.ds(pl.multiple_of(i * 64, 64), 64)
        for acc in accs:
            acc[rows, :] = jnp.zeros((64, 128), F32)
        return carry

    lax.fori_loop(0, G // 64, clear, 0)

    def add(i, carry):
        src = i // (PAIRS // STEP)
        block = i % (PAIRS // STEP)
        base = src * SLOT + block * STEP
        rows = in_ref[src, pl.ds(pl.multiple_of(block * STEP, STEP), STEP), :]
        for t in range(STEP):
            for half in range(2):
                acc = accs[(2 * t + half) % CHAINS]
                at = pl.ds(ids_ref[base + half * PAIRS + t], 1)
                acc[at, :] = acc[at, :] + rows[t : t + 1]
        return carry

    lax.fori_loop(0, N_BASE * PAIRS // STEP, add, 0)

    def total(half, rows):
        parts = [acc[rows, :] for acc in accs[half::2]]
        while len(parts) > 1:
            parts = [x + y for x, y in zip(parts[::2], parts[1::2])]
        return parts[0]

    low_half = lax.broadcasted_iota(jnp.int32, (K_TILES, 128), 1) < 64

    def rows_of(pair, carry):
        one = pl.ds(pl.multiple_of(pair * (2 * K_TILES), K_TILES), K_TILES)
        two = pl.ds(pl.multiple_of(pair * (2 * K_TILES) + K_TILES, K_TILES), K_TILES)
        a1, a2 = total(0, one), total(0, two)
        b1, b2 = total(1, one), total(1, two)
        held = jnp.where(low_half, a1, b2) + pltpu.roll(jnp.where(low_half, a2, b1), 64, 1)
        hh, hl = split(held.T)
        prod = mm3(hh, hl, eh_ref[...], el_ref[...])
        parts = []
        for t in range(2):
            re, im = prod[64 * t : 64 * t + 32], prod[64 * t + 32 : 64 * t + 64]
            y_re = re[:, 0:256] - im[:, 256:512]
            y_im = re[:, 256:512] + im[:, 0:256]
            parts.append(y_re * tc_ref[...] - y_im * ts_ref[...])
            parts.append(y_re * ts_ref[...] + y_im * tc_ref[...])
        vh, vl = split(jnp.concatenate(parts, 0))
        z = mm3(fh_ref[...], fl_ref[...], vh, vl)
        for half in range(2):
            z_ref[half, pl.ds(pl.multiple_of(pair * 128, 128), 128), :] = z[:, 128 * half : 128 * half + 128]
        return carry

    lax.fori_loop(0, TILE // 2, rows_of, 0, unroll=4)

    quarter = lax.broadcasted_iota(jnp.int32, (16, 128), 1) // 32

    def send(b2, carry):
        for half in range(2):
            parts = [z_ref[half, pl.ds(c * 32 + b2, 32, stride=64), :] for c in range(2)]
            pieces = [parts[c][16 * r : 16 * r + 16] for r in range(2) for c in range(2)]
            for zq in range(4):
                block = None
                for p in range(4):
                    moved = pieces[p] if p == zq else pltpu.roll(pieces[p], (p - zq) * 32 % 128, 1)
                    block = moved if block is None else jnp.where(quarter == p, moved, block)
                out_ref[b2 * N_BAND + half * 4 + zq] = block
        return carry

    lax.fori_loop(0, N_BASE, send, 0, unroll=4)


def row_tables():
    span = np.arange(K_TILES)
    c, s = waves(span, span, K_TILES)
    e = np.concatenate([c, s], 1)
    kx = np.arange(TILE)
    tc, ts = waves(kx, span, G)
    c32, s32 = waves(kx, kx, TILE)
    f = np.kron(np.eye(2), np.block([[c32, -s32], [s32, c32]]))
    return split_np(e) + (tc.astype(np.float32), ts.astype(np.float32)) + split_np(f)


def column_kernel(in_ref, eh_ref, el_ref, tc_ref, ts_ref, fh_ref, fl_ref, out_ref, v_ref, x_ref):
    def first(group, carry):
        lefts = []
        for t in range(4):
            block = in_ref[pl.ds((group * 4 + t) * N_BAND, N_BAND)].reshape(128, 128)
            turned = block.T
            lefts.append(jnp.concatenate([turned[0:64], turned[64:128]], 1))
        dh, dl = split(jnp.concatenate(lefts, 0))
        prod = mm3(dh, dl, eh_ref[...], el_ref[...])
        for t in range(4):
            j = group * 4 + t
            re, im = prod[64 * t : 64 * t + 32], prod[64 * t + 32 : 64 * t + 64]
            y_re = re[:, 0:256] - im[:, 256:512]
            y_im = re[:, 256:512] + im[:, 0:256]
            tc = tc_ref[pl.ds(j, 1), :]
            ts = ts_ref[pl.ds(j, 1), :]
            v_re = y_re * tc - y_im * ts
            v_im = y_re * ts + y_im * tc
            for half in range(2):
                lanes = slice(128 * half, 128 * half + 128)
                v_ref[half, pl.ds(j, 32, stride=64), :] = v_re[:, lanes]
                v_ref[half, pl.ds(32 + j, 32, stride=64), :] = v_im[:, lanes]
        return carry

    lax.fori_loop(0, N_BASE // 4, first, 0, unroll=8)

    def second(b, carry):
        rows = pl.ds(pl.multiple_of(b * 64, 64), 64)
        vh, vl = split(jnp.concatenate([v_ref[0, rows, :], v_ref[1, rows, :]], 1))
        x = mm3(fh_ref[...], fl_ref[...], vh, vl)
        for half in range(2):
            x_ref[half, rows, :] = x[:, 128 * half : 128 * half + 128]
        return carry

    lax.fori_loop(0, TILE, second, 0, unroll=16)
    for c in range(2):
        for a2 in range(TILE):
            for half in range(2):
                at = a2 * 256 + half * 128
                out_ref[c, :, at : at + 128] = x_ref[half, pl.ds(c * 32 + a2, 32, stride=64), :]


def column_tables():
    zs, rp, rpp = np.arange(8), np.arange(16), np.arange(2)
    r = (rpp[:, None, None] * 16 + zs[None, :, None] * 32 + rp[None, None, :]).reshape(-1)
    span = np.arange(K_TILES)
    c, s = waves(r, span, K_TILES)
    e = np.concatenate([c, s], 1)
    ky = np.arange(TILE)
    tc, ts = waves(ky, span, G)
    c32, s32 = waves(ky, ky, TILE)
    f = np.block([[c32, -s32], [s32, c32]]) / G
    return split_np(e) + (tc.astype(np.float32), ts.astype(np.float32)) + split_np(f)


VMEM = pl.BlockSpec(memory_space=pltpu.VMEM)
SMEM = pl.BlockSpec(memory_space=pltpu.SMEM)
LIMIT = pltpu.CompilerParams(vmem_limit_bytes=56 * 2**20)


def shards(visibilities, coords, chan_scale, taper_gain, owner_base, tile_cell):
    places = (coords[:, :, :, None] * chan_scale).reshape(SLOT, 2, 128) * (1.0 / TILE)
    ids = (tile_cell // 8) * K_TILES + owner_base[:, 0] * 8 + tile_cell % 8
    ids = ids.reshape(PAIRS, 2).T.astype(F32)
    ids = jnp.concatenate([ids, jnp.zeros((6, PAIRS), F32)], 0)
    taper = jnp.tile(taper_gain, (1, 4))
    arrived = pl.pallas_call(
        grid_kernel,
        out_shape=jax.ShapeDtypeStruct((N_BASE, ROWS, 128), F32),
        in_specs=[VMEM] * 10,
        out_specs=pl.BlockSpec(memory_space=pl.ANY),
        scratch_shapes=[
            pltpu.VMEM((8, SLOT, 128), F32),
            pltpu.VMEM((TILE * ROWS, 128), F32),
            pltpu.SemaphoreType.DMA,
            pltpu.SemaphoreType.DMA,
            pltpu.SemaphoreType.DMA,
        ],
        compiler_params=pltpu.CompilerParams(vmem_limit_bytes=56 * 2**20, collective_id=0, has_side_effects=True),
        name="gridding",
    )(
        visibilities[:, 0, :],
        visibilities[:, 1, :],
        places[:, 0, :],
        places[:, 1, :],
        ids,
        taper,
        *[jnp.asarray(t) for t in grid_tables()],
    )
    where = arrived[:, PAIRS : PAIRS + 2, :].astype(jnp.int32).reshape(N_BASE * SLOT)
    rows = pl.pallas_call(
        row_kernel,
        out_shape=jax.ShapeDtypeStruct((N_BASE * N_BAND, 16, 128), F32),
        in_specs=[SMEM] + [VMEM] * 7,
        out_specs=VMEM,
        scratch_shapes=[
            pltpu.VMEM((2, TILE * 64, 128), F32),
            *[pltpu.VMEM((G, 128), F32)] * CHAINS,
        ],
        compiler_params=LIMIT,
        name="rows",
    )(where, arrived, *[jnp.asarray(t) for t in row_tables()])
    turned = lax.all_to_all(rows, ("base", "band"), split_axis=0, concat_axis=0, tiled=True)
    return pl.pallas_call(
        column_kernel,
        out_shape=jax.ShapeDtypeStruct((2, TILE, G), F32),
        in_specs=[VMEM] * 7,
        out_specs=VMEM,
        scratch_shapes=[pltpu.VMEM((2, TILE * 64, 128), F32), pltpu.VMEM((2, TILE * 64, 128), F32)],
        compiler_params=LIMIT,
        name="columns",
    )(turned, *[jnp.asarray(t) for t in column_tables()])


def solution(mesh):
    placed = (
        P(("base", "band"), None, None),
        P(("base", "band"), None, None),
        P(),
        P(),
        P(("base", "band"), None),
        P(("base", "band")),
    )
    return jax.shard_map(
        shards,
        mesh=mesh,
        in_specs=placed,
        out_specs=P(None, ("base", "band"), None),
        check_vma=False,
    )
```

```python
import functools
import math

import jax
import jax.numpy as jnp
import ml_dtypes
import numpy as np
from jax import lax
from jax.experimental import pallas as pl
from jax.experimental.pallas import tpu as pltpu
from jax.sharding import PartitionSpec as P

G = 8192
TILE = 32
SLOT = 256
PAIRS = SLOT // 2
N_BASE = 32
N_BAND = 8
K_TILES = G // TILE
ROWS = PAIRS + 8
F32 = jnp.float32
BF16 = jnp.bfloat16


def split_np(table):
    table = np.asarray(table, np.float64)
    high = table.astype(np.float32).astype(ml_dtypes.bfloat16)
    low = (table - high.astype(np.float64)).astype(np.float32).astype(ml_dtypes.bfloat16)
    return high, low


def waves(first, second, length):
    turns = np.outer(np.asarray(first), np.asarray(second)) % length
    angle = 2.0 * np.pi / length * turns
    return np.cos(angle), np.sin(angle)


def split(x):
    high = x.astype(BF16)
    low = (x - high.astype(F32)).astype(BF16)
    return high, low


def mm(a, b):
    return lax.dot_general(a, b, (((1,), (0,)), ((), ())), preferred_element_type=F32)


def mm_nt(a, b):
    return lax.dot_general(a, b, (((1,), (1,)), ((), ())), preferred_element_type=F32)


def mm3(ah, al, bh, bl):
    return mm(ah, bh) + (mm(al, bh) + mm(ah, bl))


def fit_waves():
    r = 0.5 * np.cos(np.pi * (np.arange(4000) + 0.5) / 4000)
    odd = np.stack([r ** (2 * i + 1) for i in range(7)], 1)
    even = np.stack([r ** (2 * i) for i in range(8)], 1)
    s = np.linalg.lstsq(odd, np.sin(2 * np.pi * r), rcond=None)[0]
    c = np.linalg.lstsq(even, np.cos(2 * np.pi * r), rcond=None)[0]
    return [float(np.float32(v)) for v in s], [float(np.float32(v)) for v in c]


SIN_C, COS_C = fit_waves()


def cos_sin_turns(turns):
    r = turns - jnp.floor(turns + 0.5)
    r2 = r * r
    s = jnp.full_like(r, SIN_C[-1])
    for v in SIN_C[-2::-1]:
        s = s * r2 + v
    c = jnp.full_like(r, COS_C[-1])
    for v in COS_C[-2::-1]:
        c = c * r2 + v
    return c, s * r


UNIT = 32
SENDS = 4
MESH = pl.DeviceIdType.MESH
OFFSETS = sorted(
    [(x, y, c) for x in range(4) for y in range(4) for c in range(2) if (x, y, c) != (0, 0, 0)],
    key=lambda d: ((d[0] + d[1]) % 4, d[0], d[2]),
)


def moved(base, offset):
    x, y, c = base // 8, base // 2 % 4, base % 2
    return (x + offset[0]) % 4 * 8 + (y + offset[1]) % 4 * 2 + (c + offset[2]) % 2
CHAINS = 8
STEP = 64


def powers(base, w8, w16):
    c, s = base
    c8, s8 = w8
    c16, s16 = w16
    return [
        (c * c16 + s * s16, s * c16 - c * s16),
        (c * c8 + s * s8, s * c8 - c * s8),
        (c, s),
        (c * c8 - s * s8, s * c8 + c * s8),
    ]


def spread(values, table):
    high = values.astype(BF16)
    rest = values - high.astype(F32)
    mid = rest.astype(BF16)
    low = (rest - mid.astype(F32)).astype(BF16)
    return mm(high, table) + mm(mid, table) + mm(low, table)


def grid_kernel(
    vis_ref, coords_ref, chan_ref, ids_ref, taper_in_ref, time_ref, chan_at_ref, tile_at_ref,
    kxh_ref, kxl_ref, fyh_ref, fyl_ref,
    all_ref, w_ref, out_ref, places_ref, taper_ref, send_sem, recv_sem, own_sem,
):
    base, band = lax.axis_index("base"), lax.axis_index("band")
    barrier = pltpu.get_barrier_semaphore()
    for offset in OFFSETS:
        pl.semaphore_signal(barrier, inc=1, device_id=(moved(base, offset), band), device_id_type=MESH)
    step8 = lax.broadcasted_iota(jnp.int32, (8, 128), 0).astype(F32)
    lane = lax.broadcasted_iota(jnp.int32, (32, 128), 1)
    taper_ref[...] = spread(taper_in_ref[...], tile_at_ref[...])
    scale = spread(jnp.broadcast_to(chan_ref[...], (8, 16)), chan_at_ref[...])[0:1] * (1.0 / TILE)
    for j in range(0, SLOT, 64):
        rows = pl.ds(j, 64)
        both = spread(coords_ref[rows, :], time_ref[...])
        for i in range(2):
            turns = both[:, 128 * i : 128 * i + 128] * scale
            places_ref[i, rows, :] = turns
            c8, s8 = cos_sin_turns(turns * 8.0)
            w_ref[4 * i, rows, :] = c8
            w_ref[4 * i + 1, rows, :] = s8
            w_ref[4 * i + 2, rows, :] = c8 * c8 - s8 * s8
            w_ref[4 * i + 3, rows, :] = 2.0 * (c8 * s8)
    ids_pad = jnp.concatenate([ids_ref[...], jnp.zeros((6, 128), F32)], 0)
    for k in range(TILE):
        out_ref[pl.ds(k * ROWS + PAIRS, 8), :] = ids_pad

    def one(s):
        row = pl.ds(s, 1)

        def phases(side, first):
            turns = places_ref[side, row, :] * step8
            w = [jnp.broadcast_to(w_ref[first + i, row, :], (8, 128)) for i in range(4)]
            return powers(cos_sin_turns(turns), (w[0], w[1]), (w[2], w[3]))

        x_side = phases(0, 0)
        y_side = phases(1, 4)
        vr = jnp.broadcast_to(vis_ref[s, 0:1, :], (8, 128))
        vi = jnp.broadcast_to(vis_ref[s, 1:2, :], (8, 128))
        l_re = jnp.concatenate([vr * c - vi * s for c, s in y_side], 0)
        l_im = jnp.concatenate([vr * s + vi * c for c, s in y_side], 0)
        c_x = jnp.concatenate([c for c, s in x_side], 0)
        s_x = jnp.concatenate([s for c, s in x_side], 0)
        lrh, lrl = split(l_re)
        lih, lil = split(l_im)
        ch, cl = split(c_x)
        sh, sl = split(s_x)
        left = jnp.concatenate([jnp.concatenate([lrh, lih], 1), jnp.concatenate([lrl, lil], 1)], 0)
        right_h = jnp.concatenate([jnp.concatenate([ch, -sh], 1), jnp.concatenate([sh, ch], 1)], 0)
        right_l = jnp.concatenate([jnp.concatenate([cl, -sl], 1), jnp.concatenate([sl, cl], 1)], 0)
        return left, right_h, right_l

    def body(step, carry):
        first = step * (UNIT // 2)
        pixels = []
        for pair in range(UNIT // 2):
            a, b = one(first + pair), one(PAIRS + first + pair)
            left_h = jnp.concatenate([a[0][0:32], b[0][0:32]], 0)
            left_l = jnp.concatenate([a[0][32:64], b[0][32:64]], 0)
            right_h = jnp.concatenate([a[1], b[1]], 0)
            right_l = jnp.concatenate([a[2], b[2]], 0)
            prod = mm_nt(left_h, right_h) + (mm_nt(left_l, right_h) + mm_nt(left_h, right_l))
            pixels.append(jnp.where(lane < 64, prod[0:32], prod[32:64]) * taper_ref[...])
        ph, pl_ = split(jnp.concatenate(pixels, 0))
        q = mm3(ph, pl_, kxh_ref[...], kxl_ref[...])
        for pair in range(UNIT // 2):
            rows = slice(pair * 32, pair * 32 + 32)
            col = jnp.concatenate([q[rows, 0:128], q[rows, 128:256]], 0)
            qh, ql = split(col)
            tile = mm(fyh_ref[...], qh) + (mm(fyl_ref[...], qh) + mm(fyh_ref[...], ql))
            out_ref[pl.ds(first + pair, 32, stride=ROWS), :] = tile
        return carry

    steps = SLOT // UNIT // SENDS

    def send(part, rows):
        for offset in OFFSETS:
            to = moved(base, offset)
            pltpu.make_async_remote_copy(
                src_ref=out_ref.at[pl.ds(pl.multiple_of(to * ROWS + part, 8), rows), :],
                dst_ref=all_ref.at[base, pl.ds(pl.multiple_of(part, 8), rows), :],
                send_sem=send_sem,
                recv_sem=recv_sem,
                device_id=(to, band),
                device_id_type=MESH,
            ).start()

    rows = PAIRS // SENDS
    lax.fori_loop(0, steps, body, 0)
    pl.semaphore_wait(barrier, len(OFFSETS))
    send(0, rows)

    def later(part, carry):
        lax.fori_loop(part * steps, part * steps + steps, body, 0)
        send(part * rows, rows)
        return carry

    lax.fori_loop(1, SENDS - 1, later, 0)
    lax.fori_loop(SLOT // UNIT - steps, SLOT // UNIT, body, 0)
    send(PAIRS - rows, rows + 8)
    own = pltpu.make_async_copy(out_ref.at[pl.ds(pl.multiple_of(base * ROWS, 8), ROWS), :], all_ref.at[base], own_sem)
    own.start()
    own.wait()
    sent = out_ref.at[pl.ds(0, len(OFFSETS) * ROWS), :]
    pltpu.make_async_copy(sent, sent, send_sem).wait()
    arrived = all_ref.at[pl.ds(0, len(OFFSETS))]
    pltpu.make_async_copy(arrived, arrived, recv_sem).wait()


def grid_tables():
    span = np.arange(TILE)
    c, s = waves(span, span, TILE)
    eye2 = np.eye(2)
    fx = np.block([[c, -s], [s, c]])
    fx_turned = np.block([[-s, -c], [c, -s]])
    kx = np.concatenate([np.kron(eye2, fx), np.kron(eye2, fx_turned)], 1)
    fy = np.concatenate([c, s], 1) / (TILE * math.sqrt(128.0))
    q = np.arange(128)
    time_at = np.equal.outer(np.arange(16), np.concatenate([q // 16, 8 + q // 16]))
    chan_at = np.equal.outer(np.arange(16), q % 16)
    tile_at = np.equal.outer(span, q % TILE)
    ones = tuple(t.astype(np.float32).astype(ml_dtypes.bfloat16) for t in (time_at, chan_at, tile_at))
    return ones + split_np(kx) + split_np(fy)


def row_kernel(ids_ref, in_ref, held_ref, *accs):
    def clear(i, carry):
        rows = pl.ds(pl.multiple_of(i * 64, 64), 64)
        for acc in accs:
            acc[rows, :] = jnp.zeros((64, 128), F32)
        return carry

    lax.fori_loop(0, G // 64, clear, 0)

    def add(i, carry):
        src = i // (PAIRS // STEP)
        block = i % (PAIRS // STEP)
        base = src * SLOT + block * STEP
        rows = in_ref[src, pl.ds(pl.multiple_of(block * STEP, STEP), STEP), :]
        for t in range(STEP):
            for half in range(2):
                acc = accs[(2 * t + half) % CHAINS]
                at = pl.ds(ids_ref[base + half * PAIRS + t], 1)
                acc[at, :] = acc[at, :] + rows[t : t + 1]
        return carry

    lax.fori_loop(0, N_BASE * PAIRS // STEP, add, 0)

    def total(half, rows):
        parts = [acc[rows, :] for acc in accs[half::2]]
        while len(parts) > 1:
            parts = [x + y for x, y in zip(parts[::2], parts[1::2])]
        return parts[0]

    low_half = lax.broadcasted_iota(jnp.int32, (K_TILES, 128), 1) < 64

    def rows_of(pair, carry):
        one = pl.ds(pl.multiple_of(pair * K_TILES, K_TILES), K_TILES)
        two = pl.ds(pl.multiple_of((pair + 16) * K_TILES, K_TILES), K_TILES)
        a1, a2 = total(0, one), total(0, two)
        b1, b2 = total(1, one), total(1, two)
        held_ref[one, :] = jnp.where(low_half, a1, b2) + pltpu.roll(jnp.where(low_half, a2, b1), 64, 1)
        return carry

    lax.fori_loop(0, TILE // 2, rows_of, 0)


def row_tables():
    span = np.arange(K_TILES)
    c, s = waves(span, span, K_TILES)
    e = np.concatenate([c, s], 1)
    kx = np.arange(TILE)
    tc, ts = waves(kx, span, G)
    c32, s32 = waves(kx, kx, TILE)
    f = np.kron(np.eye(2), np.block([[c32, -s32], [s32, c32]]))
    return split_np(e) + (tc.astype(np.float32), ts.astype(np.float32)) + split_np(f)


TURNS = (2, 1, 3, 0)


def wait_for(ref, sem):
    pltpu.make_async_copy(ref, ref, sem).wait()


def send_to(source, target, send_sem, recv_sem, device):
    pltpu.make_async_remote_copy(
        src_ref=source,
        dst_ref=target,
        send_sem=send_sem,
        recv_sem=recv_sem,
        device_id=device,
        device_id_type=MESH,
    ).start()


def exchange_kernel(
    held_ref, reh_ref, rel_ref, rtc_ref, rts_ref, rfh_ref, rfl_ref, eh_ref, el_ref, tc_ref, ts_ref,
    v_ref, z_ref, out_ref, mid_ref, in_ref, send_sem, mid_sem, recv_sem, own_sem,
):
    base, band = lax.axis_index("base"), lax.axis_index("band")
    my_x, my_y, my_core = base // 8, base // 2 % 4, base % 2
    barrier = pltpu.get_barrier_semaphore()
    for step in range(1, N_BAND):
        pl.semaphore_signal(barrier, inc=1, device_id=(base, (band + step) % N_BAND), device_id_type=MESH)
    for offset in OFFSETS:
        pl.semaphore_signal(barrier, inc=1, device_id=(moved(base, offset), band), device_id_type=MESH)

    quarter = lax.broadcasted_iota(jnp.int32, (8, 128), 1) // 32

    def transform(pair, carry):
        hh, hl = split(held_ref[pl.ds(pl.multiple_of(pair * K_TILES, K_TILES), K_TILES), :].T)
        prod = mm3(hh, hl, reh_ref[...], rel_ref[...])
        parts = []
        for t in range(2):
            re, im = prod[64 * t : 64 * t + 32], prod[64 * t + 32 : 64 * t + 64]
            y_re = re[:, 0:256] - im[:, 256:512]
            y_im = re[:, 256:512] + im[:, 0:256]
            parts.append(y_re * rtc_ref[...] - y_im * rts_ref[...])
            parts.append(y_re * rts_ref[...] + y_im * rtc_ref[...])
        vh, vl = split(jnp.concatenate(parts, 0))
        z = mm3(rfh_ref[...], rfl_ref[...], vh, vl)
        for half in range(2):
            z_ref[half, pl.ds(pl.multiple_of(pair * 128, 128), 128), :] = z[:, 128 * half : 128 * half + 128]
        return carry

    def blocks(part, to_y):
        def one(i, carry):
            x, core = i // 2, i % 2
            b2 = x * 8 + to_y * 2 + core
            for half in range(2):
                pieces = [z_ref[half, pl.ds(part * 1024 + p * 32 + b2, 8, stride=128), :] for p in range(4)]
                for zq in range(4):
                    block = None
                    for p in range(4):
                        turned = pieces[p] if p == zq else pltpu.roll(pieces[p], (p - zq) * 32 % 128, 1)
                        block = turned if block is None else jnp.where(quarter == p, turned, block)
                    out_ref[x, to_y, core, half * 4 + zq, 8 * part : 8 * part + 8, :] = block
            return carry

        lax.fori_loop(0, 8, one, 0, unroll=4)

    def over_band(part, k):
        to_y = (my_y + TURNS[k]) % 4
        rows = pl.ds(8 * part, 8)
        blocks(part, to_y)
        if part + k == 0:
            pl.semaphore_wait(barrier, N_BAND - 1 + len(OFFSETS))
        for step in (4, 3, 5, 2, 6, 1, 7):
            to = (band + step) % N_BAND
            send_to(
                out_ref.at[:, to_y, :, to, rows, :],
                mid_ref.at[:, to_y, :, band, rows, :],
                send_sem,
                mid_sem.at[4 * part + k],
                (base, to),
            )
        own = pltpu.make_async_copy(
            out_ref.at[:, to_y, :, band, rows, :], mid_ref.at[:, to_y, :, band, rows, :], own_sem.at[4 * part + k]
        )
        own.start()
        own_mid.append(own)

    def over_base(part, k):
        to_y = (my_y + TURNS[k]) % 4
        rows = pl.ds(8 * part, 8)
        own_mid[4 * part + k].wait()
        wait_for(out_ref.at[:, 0, :, pl.ds(0, N_BAND - 1), rows, :], mid_sem.at[4 * part + k])
        for x in range(4):
            for core in range(2):
                held = mid_ref.at[(my_x + x) % 4, to_y, (my_core + core) % 2, :, rows, :]
                target = in_ref.at[base, :, rows, :]
                if (x, TURNS[k], core) == (0, 0, 0):
                    own = pltpu.make_async_copy(held, target, own_sem.at[8 + part])
                    own.start()
                    own_in.append(own)
                else:
                    to = (moved(base, (x, TURNS[k], core)), band)
                    send_to(held, target, send_sem, recv_sem.at[4 * part + k], to)

    def first(k):
        for part in range(2):
            count = 7 if TURNS[k] == 0 else 8
            wait_for(in_ref.at[pl.ds(0, count), :, pl.ds(8 * part, 8), :], recv_sem.at[4 * part + k])
            if TURNS[k] == 0:
                own_in[part].wait()
        from_y = (my_y - TURNS[k] + 4) % 4

        def group(g, carry):
            ids = [(2 * g + t // 2) * 8 + from_y * 2 + t % 2 for t in range(4)]
            lefts = []
            for j in ids:
                turned = in_ref[j].reshape(128, 128).T
                lefts.append(jnp.concatenate([turned[0:64], turned[64:128]], 1))
            dh, dl = split(jnp.concatenate(lefts, 0))
            prod = mm3(dh, dl, eh_ref[...], el_ref[...])
            for t, j in enumerate(ids):
                re, im = prod[64 * t : 64 * t + 32], prod[64 * t + 32 : 64 * t + 64]
                y_re = re[:, 0:256] - im[:, 256:512]
                y_im = re[:, 256:512] + im[:, 0:256]
                tc = tc_ref[pl.ds(j, 1), :]
                ts = ts_ref[pl.ds(j, 1), :]
                v_re = y_re * tc - y_im * ts
                v_im = y_re * ts + y_im * tc
                for half in range(2):
                    lanes = slice(128 * half, 128 * half + 128)
                    v_ref[half, pl.ds(j, 32, stride=64), :] = v_re[:, lanes]
                    v_ref[half, pl.ds(32 + j, 32, stride=64), :] = v_im[:, lanes]
            return carry

        lax.fori_loop(0, 2, group, 0, unroll=2)

    own_mid, own_in = [], []
    for part in range(2):
        lax.fori_loop(8 * part, 8 * part + 8, transform, 0, unroll=4)
        for k in range(4):
            over_band(part, k)
    for k in range(4):
        over_base(0, k)
    over_base(1, 0)
    over_base(1, 1)
    first(0)
    over_base(1, 2)
    first(1)
    over_base(1, 3)
    first(2)
    first(3)
    wait_for(in_ref.at[pl.ds(0, 28)], send_sem)
    wait_for(in_ref.at[pl.ds(0, 31)], send_sem)


def column_kernel(v_ref, fh_ref, fl_ref, out_ref, x_ref):
    def second(b, carry):
        rows = pl.ds(pl.multiple_of(b * 64, 64), 64)
        vh, vl = split(jnp.concatenate([v_ref[0, rows, :], v_ref[1, rows, :]], 1))
        x = mm3(fh_ref[...], fl_ref[...], vh, vl)
        for half in range(2):
            x_ref[half, rows, :] = x[:, 128 * half : 128 * half + 128]
        return carry

    lax.fori_loop(0, TILE, second, 0, unroll=16)
    for c in range(2):
        for a2 in range(TILE):
            for half in range(2):
                at = a2 * 256 + half * 128
                out_ref[c, :, at : at + 128] = x_ref[half, pl.ds(c * 32 + a2, 32, stride=64), :]


def column_tables():
    zs, rp, rpp = np.arange(8), np.arange(16), np.arange(2)
    r = (rpp[:, None, None] * 16 + zs[None, :, None] * 32 + rp[None, None, :]).reshape(-1)
    span = np.arange(K_TILES)
    c, s = waves(r, span, K_TILES)
    e = np.concatenate([c, s], 1)
    ky = np.arange(TILE)
    tc, ts = waves(ky, span, G)
    c32, s32 = waves(ky, ky, TILE)
    f = np.block([[c32, -s32], [s32, c32]]) / G
    return split_np(e) + (tc.astype(np.float32), ts.astype(np.float32)) + split_np(f)


VMEM = pl.BlockSpec(memory_space=pltpu.VMEM)
SMEM = pl.BlockSpec(memory_space=pltpu.SMEM)
LIMIT = pltpu.CompilerParams(vmem_limit_bytes=56 * 2**20)


def shards(visibilities, coords, chan_scale, taper_gain, owner_base, tile_cell):
    ids = (tile_cell // 8) * K_TILES + owner_base.reshape(SLOT) * 8 + tile_cell % 8
    ids = ids.astype(F32).reshape(2, PAIRS)
    arrived = pl.pallas_call(
        grid_kernel,
        out_shape=jax.ShapeDtypeStruct((N_BASE, ROWS, 128), F32),
        in_specs=[VMEM] * 12,
        out_specs=pl.BlockSpec(memory_space=pl.ANY),
        scratch_shapes=[
            pltpu.VMEM((8, SLOT, 128), F32),
            pltpu.VMEM((TILE * ROWS, 128), F32),
            pltpu.VMEM((2, SLOT, 128), F32),
            pltpu.VMEM((TILE, 128), F32),
            pltpu.SemaphoreType.DMA,
            pltpu.SemaphoreType.DMA,
            pltpu.SemaphoreType.DMA,
        ],
        compiler_params=pltpu.CompilerParams(vmem_limit_bytes=56 * 2**20, collective_id=0, has_side_effects=True),
        name="gridding",
    )(
        visibilities,
        coords.reshape(SLOT, 16),
        chan_scale.reshape(1, 16),
        ids,
        taper_gain,
        *[jnp.asarray(t) for t in grid_tables()],
    )
    where = arrived[:, PAIRS : PAIRS + 2, :].astype(jnp.int32).reshape(N_BASE * SLOT)
    tables = [jnp.asarray(t) for t in column_tables()]
    half_rows = pltpu.VMEM((2, TILE * 64, 128), F32)
    row_side = [jnp.asarray(t) for t in row_tables()]
    rows = pl.pallas_call(
        row_kernel,
        out_shape=jax.ShapeDtypeStruct((G // 2, 128), F32),
        in_specs=[SMEM, VMEM],
        out_specs=VMEM,
        scratch_shapes=[pltpu.VMEM((G, 128), F32)] * CHAINS,
        compiler_params=LIMIT,
        name="rows",
    )(where, arrived)
    by_target = pltpu.VMEM((4, 4, 2, N_BAND, 16, 128), F32)
    dma = pltpu.SemaphoreType.DMA
    turned = pl.pallas_call(
        exchange_kernel,
        out_shape=jax.ShapeDtypeStruct((2, TILE * 64, 128), F32),
        in_specs=[VMEM] * 11,
        out_specs=VMEM,
        scratch_shapes=[
            half_rows,
            by_target,
            by_target,
            pltpu.VMEM((N_BASE, N_BAND, 16, 128), F32),
            dma,
            dma((8,)),
            dma((8,)),
            dma((10,)),
        ],
        compiler_params=pltpu.CompilerParams(vmem_limit_bytes=56 * 2**20, collective_id=1, has_side_effects=True),
        name="exchange",
    )(rows, *row_side, *tables[:4])
    return pl.pallas_call(
        column_kernel,
        out_shape=jax.ShapeDtypeStruct((2, TILE, G), F32),
        in_specs=[VMEM] * 3,
        out_specs=VMEM,
        scratch_shapes=[half_rows],
        compiler_params=LIMIT,
        name="columns",
    )(turned, *tables[4:])


def solution(mesh):
    placed = (
        P(("base", "band"), None, None),
        P(("base", "band"), None, None),
        P(),
        P(),
        P(("base", "band"), None),
        P(("base", "band")),
    )
    return jax.shard_map(
        shards,
        mesh=mesh,
        in_specs=placed,
        out_specs=P(None, ("base", "band"), None),
        check_vma=False,
    )
```

```python
import functools
import math

import jax
import jax.numpy as jnp
import ml_dtypes
import numpy as np
from jax import lax
from jax.experimental import pallas as pl
from jax.experimental.pallas import tpu as pltpu
from jax.sharding import PartitionSpec as P

G = 8192
TILE = 32
SLOT = 256
PAIRS = SLOT // 2
N_BASE = 32
N_BAND = 8
K_TILES = G // TILE
ROWS = PAIRS + 8
F32 = jnp.float32
BF16 = jnp.bfloat16


def split_np(table):
    table = np.asarray(table, np.float64)
    high = table.astype(np.float32).astype(ml_dtypes.bfloat16)
    low = (table - high.astype(np.float64)).astype(np.float32).astype(ml_dtypes.bfloat16)
    return high, low


def waves(first, second, length):
    turns = np.outer(np.asarray(first), np.asarray(second)) % length
    angle = 2.0 * np.pi / length * turns
    return np.cos(angle), np.sin(angle)


def split(x):
    high = x.astype(BF16)
    low = (x - high.astype(F32)).astype(BF16)
    return high, low


def mm(a, b):
    return lax.dot_general(a, b, (((1,), (0,)), ((), ())), preferred_element_type=F32)


def mm_nt(a, b):
    return lax.dot_general(a, b, (((1,), (1,)), ((), ())), preferred_element_type=F32)


def mm3(ah, al, bh, bl):
    return mm(ah, bh) + (mm(al, bh) + mm(ah, bl))


def fit_waves():
    r = 0.5 * np.cos(np.pi * (np.arange(4000) + 0.5) / 4000)
    odd = np.stack([r ** (2 * i + 1) for i in range(7)], 1)
    even = np.stack([r ** (2 * i) for i in range(8)], 1)
    s = np.linalg.lstsq(odd, np.sin(2 * np.pi * r), rcond=None)[0]
    c = np.linalg.lstsq(even, np.cos(2 * np.pi * r), rcond=None)[0]
    return [float(np.float32(v)) for v in s], [float(np.float32(v)) for v in c]


SIN_C, COS_C = fit_waves()


def cos_sin_turns(turns):
    r = turns - jnp.floor(turns + 0.5)
    r2 = r * r
    s = jnp.full_like(r, SIN_C[-1])
    for v in SIN_C[-2::-1]:
        s = s * r2 + v
    c = jnp.full_like(r, COS_C[-1])
    for v in COS_C[-2::-1]:
        c = c * r2 + v
    return c, s * r


UNIT = 32
SENDS = 8
MESH = pl.DeviceIdType.MESH
OFFSETS = sorted(
    [(x, y, c) for x in range(4) for y in range(4) for c in range(2) if (x, y, c) != (0, 0, 0)],
    key=lambda d: ((d[0] + d[1]) % 4, d[0], d[2]),
)


def moved(base, offset):
    x, y, c = base // 8, base // 2 % 4, base % 2
    return (x + offset[0]) % 4 * 8 + (y + offset[1]) % 4 * 2 + (c + offset[2]) % 2
CHAINS = 8
LOADS = 4


def powers(base, w8, w16):
    c, s = base
    c8, s8 = w8
    c16, s16 = w16
    return [
        (c * c16 + s * s16, s * c16 - c * s16),
        (c * c8 + s * s8, s * c8 - c * s8),
        (c, s),
        (c * c8 - s * s8, s * c8 + c * s8),
    ]


def spread(values, table):
    high = values.astype(BF16)
    rest = values - high.astype(F32)
    mid = rest.astype(BF16)
    low = (rest - mid.astype(F32)).astype(BF16)
    return mm(high, table) + mm(mid, table) + mm(low, table)


def grid_kernel(
    vis_ref, coords_ref, chan_ref, owner_ref, cell_ref, taper_in_ref, time_ref, chan_at_ref, tile_at_ref,
    kxh_ref, kxl_ref, fyh_ref, fyl_ref,
    all_ref, w_ref, out_ref, places_ref, taper_ref, send_sem, recv_sem, own_sem,
):
    base, band = lax.axis_index("base"), lax.axis_index("band")
    barrier = pltpu.get_barrier_semaphore()
    for offset in OFFSETS:
        pl.semaphore_signal(barrier, inc=1, device_id=(moved(base, offset), band), device_id_type=MESH)
    step8 = lax.broadcasted_iota(jnp.int32, (8, 128), 0).astype(F32)
    lane = lax.broadcasted_iota(jnp.int32, (32, 128), 1)
    taper_ref[...] = spread(taper_in_ref[...], tile_at_ref[...])
    scale = spread(jnp.broadcast_to(chan_ref[...], (8, 16)), chan_at_ref[...])[0:1] * (1.0 / TILE)
    cell = cell_ref[...]
    ids = (cell >> 3) * K_TILES + owner_ref[...] * 8 + (cell & 7)
    for side in range(2):
        places_ref[side] = spread(coords_ref[side].T, time_ref[...]) * scale
    ids_pad = jnp.concatenate([ids.astype(F32), jnp.zeros((6, 128), F32)], 0)
    for k in range(TILE):
        out_ref[pl.ds(k * ROWS + PAIRS, 8), :] = ids_pad

    def one(s):
        def phases(side):
            row = pl.ds(s, 1)
            turns = places_ref[side, row, :] * step8
            w = [jnp.broadcast_to(w_ref[side, i, row, :], (8, 128)) for i in range(4)]
            return powers(cos_sin_turns(turns), (w[0], w[1]), (w[2], w[3]))

        x_side = phases(0)
        y_side = phases(1)
        vr = jnp.broadcast_to(vis_ref[s, 0:1, :], (8, 128))
        vi = jnp.broadcast_to(vis_ref[s, 1:2, :], (8, 128))
        l_re = jnp.concatenate([vr * c - vi * s for c, s in y_side], 0)
        l_im = jnp.concatenate([vr * s + vi * c for c, s in y_side], 0)
        c_x = jnp.concatenate([c for c, s in x_side], 0)
        s_x = jnp.concatenate([s for c, s in x_side], 0)
        lrh, lrl = split(l_re)
        lih, lil = split(l_im)
        ch, cl = split(c_x)
        sh, sl = split(s_x)
        left = jnp.concatenate([jnp.concatenate([lrh, lih], 1), jnp.concatenate([lrl, lil], 1)], 0)
        right_h = jnp.concatenate([jnp.concatenate([ch, -sh], 1), jnp.concatenate([sh, ch], 1)], 0)
        right_l = jnp.concatenate([jnp.concatenate([cl, -sl], 1), jnp.concatenate([sl, cl], 1)], 0)
        return left, right_h, right_l

    def body(step, carry):
        first = step * (UNIT // 2)
        for half in range(2):
            rows = pl.ds(pl.multiple_of(half * PAIRS + first, UNIT // 2), UNIT // 2)
            for side in range(2):
                c8, s8 = cos_sin_turns(places_ref[side, rows, :] * 8.0)
                w_ref[side, 0, rows, :] = c8
                w_ref[side, 1, rows, :] = s8
                w_ref[side, 2, rows, :] = c8 * c8 - s8 * s8
                w_ref[side, 3, rows, :] = 2.0 * (c8 * s8)
        pixels = []
        for pair in range(UNIT // 2):
            a, b = one(first + pair), one(PAIRS + first + pair)
            left_h = jnp.concatenate([a[0][0:32], b[0][0:32]], 0)
            left_l = jnp.concatenate([a[0][32:64], b[0][32:64]], 0)
            right_h = jnp.concatenate([a[1], b[1]], 0)
            right_l = jnp.concatenate([a[2], b[2]], 0)
            prod = mm_nt(left_h, right_h) + (mm_nt(left_l, right_h) + mm_nt(left_h, right_l))
            pixels.append(jnp.where(lane < 64, prod[0:32], prod[32:64]) * taper_ref[...])
        ph, pl_ = split(jnp.concatenate(pixels, 0))
        q = mm3(ph, pl_, kxh_ref[...], kxl_ref[...])
        for pair in range(UNIT // 2):
            rows = slice(pair * 32, pair * 32 + 32)
            col = jnp.concatenate([q[rows, 0:128], q[rows, 128:256]], 0)
            qh, ql = split(col)
            tile = mm(fyh_ref[...], qh) + (mm(fyl_ref[...], qh) + mm(fyh_ref[...], ql))
            out_ref[pl.ds(first + pair, 32, stride=ROWS), :] = tile
        return carry

    steps = SLOT // UNIT // SENDS

    def send(part, rows):
        for offset in OFFSETS:
            to = moved(base, offset)
            pltpu.make_async_remote_copy(
                src_ref=out_ref.at[pl.ds(pl.multiple_of(to * ROWS + part, 8), rows), :],
                dst_ref=all_ref.at[base, pl.ds(pl.multiple_of(part, 8), rows), :],
                send_sem=send_sem,
                recv_sem=recv_sem,
                device_id=(to, band),
                device_id_type=MESH,
            ).start()

    rows = PAIRS // SENDS
    lax.fori_loop(0, steps, body, 0)
    pl.semaphore_wait(barrier, len(OFFSETS))
    send(0, rows)

    def later(part, carry):
        lax.fori_loop(part * steps, part * steps + steps, body, 0)
        send(part * rows, rows)
        return carry

    lax.fori_loop(1, SENDS - 1, later, 0)
    lax.fori_loop(SLOT // UNIT - steps, SLOT // UNIT, body, 0)
    send(PAIRS - rows, rows + 8)
    own = pltpu.make_async_copy(out_ref.at[pl.ds(pl.multiple_of(base * ROWS, 8), ROWS), :], all_ref.at[base], own_sem)
    own.start()
    own.wait()
    sent = out_ref.at[pl.ds(0, len(OFFSETS) * ROWS), :]
    pltpu.make_async_copy(sent, sent, send_sem).wait()
    arrived = all_ref.at[pl.ds(0, len(OFFSETS))]
    pltpu.make_async_copy(arrived, arrived, recv_sem).wait()


def grid_tables():
    span = np.arange(TILE)
    c, s = waves(span, span, TILE)
    eye2 = np.eye(2)
    fx = np.block([[c, -s], [s, c]])
    fx_turned = np.block([[-s, -c], [c, -s]])
    kx = np.concatenate([np.kron(eye2, fx), np.kron(eye2, fx_turned)], 1)
    fy = np.concatenate([c, s], 1) / (TILE * math.sqrt(128.0))
    q = np.arange(128)
    time_at = np.equal.outer(np.arange(8), q // 16)
    chan_at = np.equal.outer(np.arange(16), q % 16)
    tile_at = np.equal.outer(span, q % TILE)
    ones = tuple(t.astype(np.float32).astype(ml_dtypes.bfloat16) for t in (time_at, chan_at, tile_at))
    return ones + split_np(kx) + split_np(fy)


def row_kernel(all_ref, held_ref, in_ref, out_ref, number_ref, where_ref, ids_ref, load_sem, store_sem, ids_sem, *accs):
    numbers = pltpu.make_async_copy(all_ref.at[:, pl.ds(PAIRS, 8), :], number_ref, ids_sem)
    numbers.start()
    sources = N_BASE // LOADS
    loads = []
    for i in range(LOADS):
        part = pl.ds(i * sources, sources)
        loads.append(
            pltpu.make_async_copy(all_ref.at[part, pl.ds(0, PAIRS), :], in_ref.at[part], load_sem.at[i])
        )
        loads[i].start()
    numbers.wait()
    for src in range(N_BASE):
        where_ref[2 * src : 2 * src + 2, :] = number_ref[src, 0:2, :].astype(jnp.int32)
    ids_copy = pltpu.make_async_copy(where_ref, ids_ref, ids_sem)
    ids_copy.start()

    def clear(i, carry):
        rows = pl.ds(pl.multiple_of(i * 64, 64), 64)
        for acc in accs:
            acc[rows, :] = jnp.zeros((64, 128), F32)
        return carry

    lax.fori_loop(0, G // 64, clear, 0)
    ids_copy.wait()

    def add(src, carry):
        for t in range(PAIRS):
            row = in_ref[src, t : t + 1, :]
            for half in range(2):
                acc = accs[(2 * t + half) % CHAINS]
                at = pl.ds(ids_ref[2 * src + half, t], 1)
                acc[at, :] = acc[at, :] + row
        return carry

    for i in range(LOADS):
        loads[i].wait()
        lax.fori_loop(i * sources, (i + 1) * sources, add, 0)

    def total(half, rows):
        parts = [acc[rows, :] for acc in accs[half::2]]
        while len(parts) > 1:
            parts = [x + y for x, y in zip(parts[::2], parts[1::2])]
        return parts[0]

    low_half = lax.broadcasted_iota(jnp.int32, (K_TILES, 128), 1) < 64

    def rows_of(pair, carry):
        one = pl.ds(pl.multiple_of(pair * K_TILES, K_TILES), K_TILES)
        two = pl.ds(pl.multiple_of((pair + 16) * K_TILES, K_TILES), K_TILES)
        a1, a2 = total(0, one), total(0, two)
        b1, b2 = total(1, one), total(1, two)
        out_ref[one, :] = jnp.where(low_half, a1, b2) + pltpu.roll(jnp.where(low_half, a2, b1), 64, 1)
        return carry

    stores = []
    pairs = 16 // LOADS
    for i in range(LOADS):
        lax.fori_loop(i * pairs, (i + 1) * pairs, rows_of, 0, unroll=2)
        part = pl.ds(i * pairs * K_TILES, pairs * K_TILES)
        stores.append(pltpu.make_async_copy(out_ref.at[part, :], held_ref.at[part, :], store_sem.at[i]))
        stores[i].start()
    for store in stores:
        store.wait()


def row_tables():
    span = np.arange(K_TILES)
    c, s = waves(span, span, K_TILES)
    e = np.concatenate([c, s], 1)
    kx = np.arange(TILE)
    tc, ts = waves(kx, span, G)
    c32, s32 = waves(kx, kx, TILE)
    f = np.kron(np.eye(2), np.block([[c32, -s32], [s32, c32]]))
    return split_np(e) + (tc.astype(np.float32), ts.astype(np.float32)) + split_np(f)


TURNS = (2, 1, 3, 0)


def wait_for(ref, sem):
    pltpu.make_async_copy(ref, ref, sem).wait()


def send_to(source, target, send_sem, recv_sem, device):
    pltpu.make_async_remote_copy(
        src_ref=source,
        dst_ref=target,
        send_sem=send_sem,
        recv_sem=recv_sem,
        device_id=device,
        device_id_type=MESH,
    ).start()


def exchange_kernel(
    rows_ref, reh_ref, rel_ref, rtc_ref, rts_ref, rfh_ref, rfl_ref, eh_ref, el_ref, tc_ref, ts_ref,
    v_ref, held_ref, z_ref, out_ref, mid_ref, in_ref, load_sem, send_sem, mid_sem, recv_sem, own_sem,
):
    base, band = lax.axis_index("base"), lax.axis_index("band")
    my_x, my_y, my_core = base // 8, base // 2 % 4, base % 2
    loads = []
    for i in range(4):
        part = pl.ds(i * 4 * K_TILES, 4 * K_TILES)
        loads.append(pltpu.make_async_copy(rows_ref.at[part, :], held_ref.at[part, :], load_sem.at[i]))
        loads[i].start()
    barrier = pltpu.get_barrier_semaphore()
    for step in range(1, N_BAND):
        pl.semaphore_signal(barrier, inc=1, device_id=(base, (band + step) % N_BAND), device_id_type=MESH)
    for offset in OFFSETS:
        pl.semaphore_signal(barrier, inc=1, device_id=(moved(base, offset), band), device_id_type=MESH)

    quarter = lax.broadcasted_iota(jnp.int32, (8, 128), 1) // 32

    def transform(pair, carry):
        hh, hl = split(held_ref[pl.ds(pl.multiple_of(pair * K_TILES, K_TILES), K_TILES), :].T)
        prod = mm3(hh, hl, reh_ref[...], rel_ref[...])
        parts = []
        for t in range(2):
            re, im = prod[64 * t : 64 * t + 32], prod[64 * t + 32 : 64 * t + 64]
            y_re = re[:, 0:256] - im[:, 256:512]
            y_im = re[:, 256:512] + im[:, 0:256]
            parts.append(y_re * rtc_ref[...] - y_im * rts_ref[...])
            parts.append(y_re * rts_ref[...] + y_im * rtc_ref[...])
        vh, vl = split(jnp.concatenate(parts, 0))
        z = mm3(rfh_ref[...], rfl_ref[...], vh, vl)
        for half in range(2):
            z_ref[half, pl.ds(pl.multiple_of(pair * 128, 128), 128), :] = z[:, 128 * half : 128 * half + 128]
        return carry

    def blocks(part, to_y):
        def one(i, carry):
            x, core = i // 2, i % 2
            b2 = x * 8 + to_y * 2 + core
            for half in range(2):
                pieces = [z_ref[half, pl.ds(part * 1024 + p * 32 + b2, 8, stride=128), :] for p in range(4)]
                for zq in range(4):
                    block = None
                    for p in range(4):
                        turned = pieces[p] if p == zq else pltpu.roll(pieces[p], (p - zq) * 32 % 128, 1)
                        block = turned if block is None else jnp.where(quarter == p, turned, block)
                    out_ref[x, to_y, core, half * 4 + zq, 8 * part : 8 * part + 8, :] = block
            return carry

        lax.fori_loop(0, 8, one, 0, unroll=4)

    def over_band(part, k):
        to_y = (my_y + TURNS[k]) % 4
        rows = pl.ds(8 * part, 8)
        blocks(part, to_y)
        if part + k == 0:
            pl.semaphore_wait(barrier, N_BAND - 1 + len(OFFSETS))
        for step in (4, 3, 5, 2, 6, 1, 7):
            to = (band + step) % N_BAND
            send_to(
                out_ref.at[:, to_y, :, to, rows, :],
                mid_ref.at[:, to_y, :, band, rows, :],
                send_sem,
                mid_sem.at[4 * part + k],
                (base, to),
            )
        own = pltpu.make_async_copy(
            out_ref.at[:, to_y, :, band, rows, :], mid_ref.at[:, to_y, :, band, rows, :], own_sem.at[4 * part + k]
        )
        own.start()
        own_mid.append(own)

    def over_base(part, k):
        to_y = (my_y + TURNS[k]) % 4
        rows = pl.ds(8 * part, 8)
        own_mid[4 * part + k].wait()
        wait_for(out_ref.at[:, 0, :, pl.ds(0, N_BAND - 1), rows, :], mid_sem.at[4 * part + k])
        for x in range(4):
            for core in range(2):
                held = mid_ref.at[(my_x + x) % 4, to_y, (my_core + core) % 2, :, rows, :]
                target = in_ref.at[base, :, rows, :]
                if (x, TURNS[k], core) == (0, 0, 0):
                    own = pltpu.make_async_copy(held, target, own_sem.at[8 + part])
                    own.start()
                    own_in.append(own)
                else:
                    to = (moved(base, (x, TURNS[k], core)), band)
                    send_to(held, target, send_sem, recv_sem.at[4 * part + k], to)

    def first(k):
        for part in range(2):
            count = 7 if TURNS[k] == 0 else 8
            wait_for(in_ref.at[pl.ds(0, count), :, pl.ds(8 * part, 8), :], recv_sem.at[4 * part + k])
            if TURNS[k] == 0:
                own_in[part].wait()
        from_y = (my_y - TURNS[k] + 4) % 4

        def group(g, carry):
            ids = [(2 * g + t // 2) * 8 + from_y * 2 + t % 2 for t in range(4)]
            lefts = []
            for j in ids:
                turned = in_ref[j].reshape(128, 128).T
                lefts.append(jnp.concatenate([turned[0:64], turned[64:128]], 1))
            dh, dl = split(jnp.concatenate(lefts, 0))
            prod = mm3(dh, dl, eh_ref[...], el_ref[...])
            for t, j in enumerate(ids):
                re, im = prod[64 * t : 64 * t + 32], prod[64 * t + 32 : 64 * t + 64]
                y_re = re[:, 0:256] - im[:, 256:512]
                y_im = re[:, 256:512] + im[:, 0:256]
                tc = tc_ref[pl.ds(j, 1), :]
                ts = ts_ref[pl.ds(j, 1), :]
                v_re = y_re * tc - y_im * ts
                v_im = y_re * ts + y_im * tc
                for half in range(2):
                    lanes = slice(128 * half, 128 * half + 128)
                    v_ref[half, pl.ds(j, 32, stride=64), :] = v_re[:, lanes]
                    v_ref[half, pl.ds(32 + j, 32, stride=64), :] = v_im[:, lanes]
            return carry

        lax.fori_loop(0, 2, group, 0, unroll=2)

    own_mid, own_in = [], []
    for part in range(2):
        for i in range(2 * part, 2 * part + 2):
            loads[i].wait()
            lax.fori_loop(4 * i, 4 * i + 4, transform, 0, unroll=4)
        for k in range(4):
            over_band(part, k)
    for k in range(4):
        over_base(0, k)
    over_base(1, 0)
    over_base(1, 1)
    first(0)
    over_base(1, 2)
    first(1)
    over_base(1, 3)
    first(2)
    first(3)
    wait_for(in_ref.at[pl.ds(0, 28)], send_sem)
    wait_for(in_ref.at[pl.ds(0, 31)], send_sem)


def column_kernel(v_ref, fh_ref, fl_ref, out_ref, x_ref):
    def second(b, carry):
        rows = pl.ds(pl.multiple_of(b * 64, 64), 64)
        vh, vl = split(jnp.concatenate([v_ref[0, rows, :], v_ref[1, rows, :]], 1))
        x = mm3(fh_ref[...], fl_ref[...], vh, vl)
        for half in range(2):
            x_ref[half, rows, :] = x[:, 128 * half : 128 * half + 128]
        return carry

    lax.fori_loop(0, 8, second, 0, unroll=8)
    for c in range(2):
        for a2 in range(TILE):
            for half in range(2):
                at = a2 * 256 + half * 128
                out_ref[c, :, at : at + 128] = x_ref[half, pl.ds(c * 32 + a2, 8, stride=64), :]


def column_tables():
    zs, rp, rpp = np.arange(8), np.arange(16), np.arange(2)
    r = (rpp[:, None, None] * 16 + zs[None, :, None] * 32 + rp[None, None, :]).reshape(-1)
    span = np.arange(K_TILES)
    c, s = waves(r, span, K_TILES)
    e = np.concatenate([c, s], 1)
    ky = np.arange(TILE)
    tc, ts = waves(ky, span, G)
    c32, s32 = waves(ky, ky, TILE)
    f = np.block([[c32, -s32], [s32, c32]]) / G
    return split_np(e) + (tc.astype(np.float32), ts.astype(np.float32)) + split_np(f)


VMEM = pl.BlockSpec(memory_space=pltpu.VMEM)
HBM = pl.BlockSpec(memory_space=pl.ANY)
LIMIT = pltpu.CompilerParams(vmem_limit_bytes=56 * 2**20)


def shards(visibilities, coords, chan_scale, taper_gain, owner_base, tile_cell):
    arrived = pl.pallas_call(
        grid_kernel,
        out_shape=jax.ShapeDtypeStruct((N_BASE, ROWS, 128), F32),
        in_specs=[VMEM] * 13,
        out_specs=pl.BlockSpec(memory_space=pl.ANY),
        scratch_shapes=[
            pltpu.VMEM((2, 4, SLOT, 128), F32),
            pltpu.VMEM((TILE * ROWS, 128), F32),
            pltpu.VMEM((2, SLOT, 128), F32),
            pltpu.VMEM((TILE, 128), F32),
            pltpu.SemaphoreType.DMA,
            pltpu.SemaphoreType.DMA,
            pltpu.SemaphoreType.DMA,
        ],
        compiler_params=pltpu.CompilerParams(vmem_limit_bytes=56 * 2**20, collective_id=0, has_side_effects=True),
        name="gridding",
    )(
        visibilities,
        coords.transpose(1, 2, 0),
        chan_scale.reshape(1, 16),
        owner_base.reshape(2, PAIRS),
        tile_cell.reshape(2, PAIRS),
        taper_gain,
        *[jnp.asarray(t) for t in grid_tables()],
    )
    tables = [jnp.asarray(t) for t in column_tables()]
    half_rows = pltpu.VMEM((2, TILE * 64, 128), F32)
    row_side = [jnp.asarray(t) for t in row_tables()]
    rows = pl.pallas_call(
        row_kernel,
        out_shape=jax.ShapeDtypeStruct((G // 2, 128), F32),
        in_specs=[HBM],
        out_specs=HBM,
        scratch_shapes=[
            pltpu.VMEM((N_BASE, PAIRS, 128), F32),
            pltpu.VMEM((G // 2, 128), F32),
            pltpu.VMEM((N_BASE, 8, 128), F32),
            pltpu.VMEM((2 * N_BASE, PAIRS), jnp.int32),
            pltpu.SMEM((2 * N_BASE, PAIRS), jnp.int32),
            pltpu.SemaphoreType.DMA((LOADS,)),
            pltpu.SemaphoreType.DMA((LOADS,)),
            pltpu.SemaphoreType.DMA,
            *[pltpu.VMEM((G, 128), F32)] * CHAINS,
        ],
        compiler_params=LIMIT,
        name="rows",
    )(arrived)
    by_target = pltpu.VMEM((4, 4, 2, N_BAND, 16, 128), F32)
    dma = pltpu.SemaphoreType.DMA
    turned = pl.pallas_call(
        exchange_kernel,
        out_shape=jax.ShapeDtypeStruct((2, TILE * 64, 128), F32),
        in_specs=[HBM] + [VMEM] * 10,
        out_specs=VMEM,
        scratch_shapes=[
            pltpu.VMEM((G // 2, 128), F32),
            half_rows,
            by_target,
            by_target,
            pltpu.VMEM((N_BASE, N_BAND, 16, 128), F32),
            dma((4,)),
            dma,
            dma((8,)),
            dma((8,)),
            dma((10,)),
        ],
        compiler_params=pltpu.CompilerParams(vmem_limit_bytes=56 * 2**20, collective_id=1, has_side_effects=True),
        name="exchange",
    )(rows, *row_side, *tables[:4])
    return pl.pallas_call(
        column_kernel,
        out_shape=jax.ShapeDtypeStruct((2, TILE, G), F32),
        grid=(TILE // 8,),
        in_specs=[
            pl.BlockSpec((2, 512, 128), lambda i: (0, i, 0)),
            pl.BlockSpec((64, 64), lambda i: (0, 0)),
            pl.BlockSpec((64, 64), lambda i: (0, 0)),
        ],
        out_specs=pl.BlockSpec((2, 8, G), lambda i: (0, i, 0)),
        scratch_shapes=[pltpu.VMEM((2, 512, 128), F32)],
        compiler_params=LIMIT,
        name="columns",
    )(turned, *tables[4:])


def solution(mesh):
    placed = (
        P(("base", "band"), None, None),
        P(("base", "band"), None, None),
        P(),
        P(),
        P(("base", "band"), None),
        P(("base", "band")),
    )
    return jax.shard_map(
        shards,
        mesh=mesh,
        in_specs=placed,
        out_specs=P(None, ("base", "band"), None),
        check_vma=False,
    )
```

```python
import functools
import math

import jax
import jax.numpy as jnp
import ml_dtypes
import numpy as np
from jax import lax
from jax.experimental import pallas as pl
from jax.experimental.pallas import tpu as pltpu
from jax.sharding import PartitionSpec as P

G = 8192
TILE = 32
SLOT = 256
PAIRS = SLOT // 2
N_BASE = 32
N_BAND = 8
K_TILES = G // TILE
ROWS = PAIRS + 8
F32 = jnp.float32
BF16 = jnp.bfloat16


def split_np(table):
    table = np.asarray(table, np.float64)
    high = table.astype(np.float32).astype(ml_dtypes.bfloat16)
    low = (table - high.astype(np.float64)).astype(np.float32).astype(ml_dtypes.bfloat16)
    return high, low


def waves(first, second, length):
    turns = np.outer(np.asarray(first), np.asarray(second)) % length
    angle = 2.0 * np.pi / length * turns
    return np.cos(angle), np.sin(angle)


def split(x):
    high = x.astype(BF16)
    low = (x - high.astype(F32)).astype(BF16)
    return high, low


def mm(a, b):
    return lax.dot_general(a, b, (((1,), (0,)), ((), ())), preferred_element_type=F32)


def mm_nt(a, b):
    return lax.dot_general(a, b, (((1,), (1,)), ((), ())), preferred_element_type=F32)


def mm3(ah, al, bh, bl):
    rows = ah.shape[0]
    both = mm(jnp.concatenate([ah, al], 0), bh)
    return both[:rows] + (both[rows:] + mm(ah, bl))


def fit_waves():
    r = 0.5 * np.cos(np.pi * (np.arange(4000) + 0.5) / 4000)
    odd = np.stack([r ** (2 * i + 1) for i in range(7)], 1)
    even = np.stack([r ** (2 * i) for i in range(8)], 1)
    s = np.linalg.lstsq(odd, np.sin(2 * np.pi * r), rcond=None)[0]
    c = np.linalg.lstsq(even, np.cos(2 * np.pi * r), rcond=None)[0]
    return [float(np.float32(v)) for v in s], [float(np.float32(v)) for v in c]


SIN_C, COS_C = fit_waves()


def cos_sin_turns(turns):
    r = turns - jnp.floor(turns + 0.5)
    r2 = r * r
    s = jnp.full_like(r, SIN_C[-1])
    for v in SIN_C[-2::-1]:
        s = s * r2 + v
    c = jnp.full_like(r, COS_C[-1])
    for v in COS_C[-2::-1]:
        c = c * r2 + v
    return c, s * r


UNIT = 32
SENDS = 8
MESH = pl.DeviceIdType.MESH
OFFSETS = sorted(
    [(x, y, c) for x in range(4) for y in range(4) for c in range(2) if (x, y, c) != (0, 0, 0)],
    key=lambda d: ((d[0] + d[1]) % 4, d[0], d[2]),
)


def moved(base, offset):
    x, y, c = base // 8, base // 2 % 4, base % 2
    return (x + offset[0]) % 4 * 8 + (y + offset[1]) % 4 * 2 + (c + offset[2]) % 2
PITCH = 72
Z_PITCH = 136
CHAINS = 8
LOADS = 4


def powers(base, w8, w16):
    c, s = base
    c8, s8 = w8
    c16, s16 = w16
    return [
        (c * c16 + s * s16, s * c16 - c * s16),
        (c * c8 + s * s8, s * c8 - c * s8),
        (c, s),
        (c * c8 - s * s8, s * c8 + c * s8),
    ]


def spread(values, table):
    high = values.astype(BF16)
    rest = values - high.astype(F32)
    mid = rest.astype(BF16)
    low = (rest - mid.astype(F32)).astype(BF16)
    return mm(high, table) + mm(mid, table) + mm(low, table)


def grid_kernel(
    vis_ref, coords_ref, chan_ref, owner_ref, cell_ref, taper_in_ref, time_ref, chan_at_ref, tile_at_ref,
    kxh_ref, kxl_ref, fyh_ref, fyl_ref,
    all_ref, all_ids_ref, w_ref, out_ref, ids_ref, places_ref, taper_ref, send_sem, recv_sem, own_sem,
):
    base, band = lax.axis_index("base"), lax.axis_index("band")
    barrier = pltpu.get_barrier_semaphore()
    for offset in OFFSETS:
        pl.semaphore_signal(barrier, inc=1, device_id=(moved(base, offset), band), device_id_type=MESH)
    step8 = lax.broadcasted_iota(jnp.int32, (8, 128), 0).astype(F32)
    lane = lax.broadcasted_iota(jnp.int32, (32, 128), 1)
    taper_ref[...] = spread(taper_in_ref[...], tile_at_ref[...])
    scale = spread(jnp.broadcast_to(chan_ref[...], (8, 16)), chan_at_ref[...])[0:1] * (1.0 / TILE)
    cell = cell_ref[...]
    ids_ref[...] = (cell >> 3) * K_TILES + owner_ref[...] * 8 + (cell & 7)
    for side in range(2):
        places_ref[side] = spread(coords_ref[side].T, time_ref[...]) * scale
    def one(s):
        def phases(side):
            row = pl.ds(s, 1)
            turns = places_ref[side, row, :] * step8
            w = [jnp.broadcast_to(w_ref[side, i, row, :], (8, 128)) for i in range(4)]
            return powers(cos_sin_turns(turns), (w[0], w[1]), (w[2], w[3]))

        x_side = phases(0)
        y_side = phases(1)
        vr = jnp.broadcast_to(vis_ref[s, 0:1, :], (8, 128))
        vi = jnp.broadcast_to(vis_ref[s, 1:2, :], (8, 128))
        l_re = jnp.concatenate([vr * c - vi * s for c, s in y_side], 0)
        l_im = jnp.concatenate([vr * s + vi * c for c, s in y_side], 0)
        c_x = jnp.concatenate([c for c, s in x_side], 0)
        s_x = jnp.concatenate([s for c, s in x_side], 0)
        lrh, lrl = split(l_re)
        lih, lil = split(l_im)
        ch, cl = split(c_x)
        sh, sl = split(s_x)
        left = jnp.concatenate([jnp.concatenate([lrh, lih], 1), jnp.concatenate([lrl, lil], 1)], 0)
        right_h = jnp.concatenate([jnp.concatenate([ch, -sh], 1), jnp.concatenate([sh, ch], 1)], 0)
        right_l = jnp.concatenate([jnp.concatenate([cl, -sl], 1), jnp.concatenate([sl, cl], 1)], 0)
        return left, right_h, right_l

    def body(step, carry):
        first = step * (UNIT // 2)
        for half in range(2):
            rows = pl.ds(pl.multiple_of(half * PAIRS + first, UNIT // 2), UNIT // 2)
            for side in range(2):
                c8, s8 = cos_sin_turns(places_ref[side, rows, :] * 8.0)
                w_ref[side, 0, rows, :] = c8
                w_ref[side, 1, rows, :] = s8
                w_ref[side, 2, rows, :] = c8 * c8 - s8 * s8
                w_ref[side, 3, rows, :] = 2.0 * (c8 * s8)
        pixels = []
        for pair in range(UNIT // 2):
            a, b = one(first + pair), one(PAIRS + first + pair)
            left_h = jnp.concatenate([a[0][0:32], b[0][0:32]], 0)
            left_l = jnp.concatenate([a[0][32:64], b[0][32:64]], 0)
            right_h = jnp.concatenate([a[1], b[1]], 0)
            right_l = jnp.concatenate([a[2], b[2]], 0)
            both = mm_nt(jnp.concatenate([left_h, left_l], 0), right_h)
            prod = both[0:64] + (both[64:128] + mm_nt(left_h, right_l))
            pixels.append(jnp.where(lane < 64, prod[0:32], prod[32:64]) * taper_ref[...])
        ph, pl_ = split(jnp.concatenate(pixels, 0))
        q = mm3(ph, pl_, kxh_ref[...], kxl_ref[...])
        for pair in range(UNIT // 2):
            rows = slice(pair * 32, pair * 32 + 32)
            col = jnp.concatenate([q[rows, 0:128], q[rows, 128:256]], 0)
            qh, ql = split(col)
            tile = mm3(fyh_ref[...], fyl_ref[...], qh, ql)
            out_ref[pl.ds(first + pair, 32, stride=ROWS), :] = tile
        return carry

    steps = SLOT // UNIT // SENDS

    def send(part, rows):
        for offset in OFFSETS:
            to = moved(base, offset)
            pltpu.make_async_remote_copy(
                src_ref=out_ref.at[pl.ds(pl.multiple_of(to * ROWS + part, 8), rows), :],
                dst_ref=all_ref.at[base, pl.ds(pl.multiple_of(part, 8), rows), :],
                send_sem=send_sem.at[0],
                recv_sem=recv_sem.at[0],
                device_id=(to, band),
                device_id_type=MESH,
            ).start()

    rows = PAIRS // SENDS
    lax.fori_loop(0, steps, body, 0)
    pl.semaphore_wait(barrier, len(OFFSETS))
    send(0, rows)
    for offset in OFFSETS:
        pltpu.make_async_remote_copy(
            src_ref=ids_ref,
            dst_ref=all_ids_ref.at[base],
            send_sem=send_sem.at[1],
            recv_sem=recv_sem.at[1],
            device_id=(moved(base, offset), band),
            device_id_type=MESH,
        ).start()

    def later(part, carry):
        lax.fori_loop(part * steps, part * steps + steps, body, 0)
        send(part * rows, rows)
        return carry

    lax.fori_loop(1, SENDS - 1, later, 0)
    lax.fori_loop(SLOT // UNIT - steps, SLOT // UNIT, body, 0)
    send(PAIRS - rows, rows)
    own = [
        pltpu.make_async_copy(
            out_ref.at[pl.ds(pl.multiple_of(base * ROWS, 8), PAIRS), :], all_ref.at[base], own_sem.at[0]
        ),
        pltpu.make_async_copy(ids_ref, all_ids_ref.at[base], own_sem.at[1]),
    ]
    for copy in own:
        copy.start()
    for copy in own:
        copy.wait()
    for i, ref in enumerate((all_ref, all_ids_ref)):
        arrived = ref.at[pl.ds(0, len(OFFSETS))]
        pltpu.make_async_copy(arrived, arrived, send_sem.at[i]).wait()
        pltpu.make_async_copy(arrived, arrived, recv_sem.at[i]).wait()


def grid_tables():
    span = np.arange(TILE)
    c, s = waves(span, span, TILE)
    eye2 = np.eye(2)
    fx = np.block([[c, -s], [s, c]])
    fx_turned = np.block([[-s, -c], [c, -s]])
    kx = np.concatenate([np.kron(eye2, fx), np.kron(eye2, fx_turned)], 1)
    fy = np.concatenate([c, s], 1) / (TILE * math.sqrt(128.0))
    q = np.arange(128)
    time_at = np.equal.outer(np.arange(8), q // 16)
    chan_at = np.equal.outer(np.arange(16), q % 16)
    tile_at = np.equal.outer(span, q % TILE)
    ones = tuple(t.astype(np.float32).astype(ml_dtypes.bfloat16) for t in (time_at, chan_at, tile_at))
    return ones + split_np(kx) + split_np(fy)


def row_kernel(all_ref, all_ids_ref, held_ref, in_ref, out_ref, ids_ref, load_sem, store_sem, ids_sem, *accs):
    ids_copy = pltpu.make_async_copy(all_ids_ref, ids_ref, ids_sem)
    ids_copy.start()
    sources = N_BASE // LOADS
    loads = []
    for i in range(LOADS):
        part = pl.ds(i * sources, sources)
        loads.append(
            pltpu.make_async_copy(all_ref.at[part], in_ref.at[part], load_sem.at[i])
        )
        loads[i].start()
    def clear(i, carry):
        rows = pl.ds(pl.multiple_of(i * 64, 64), 64)
        for acc in accs:
            acc[rows, :] = jnp.zeros((64, 128), F32)
        return carry

    lax.fori_loop(0, G // 64, clear, 0)
    ids_copy.wait()

    def add(src, carry):
        for t in range(PAIRS):
            row = in_ref[src, t : t + 1, :]
            for half in range(2):
                acc = accs[(2 * t + half) % CHAINS]
                at = pl.ds(ids_ref[src, half, t], 1)
                acc[at, :] = acc[at, :] + row
        return carry

    for i in range(LOADS):
        loads[i].wait()
        lax.fori_loop(i * sources, (i + 1) * sources, add, 0)

    def total(half, rows):
        parts = [acc[rows, :] for acc in accs[half::2]]
        while len(parts) > 1:
            parts = [x + y for x, y in zip(parts[::2], parts[1::2])]
        return parts[0]

    low_half = lax.broadcasted_iota(jnp.int32, (K_TILES, 128), 1) < 64

    def rows_of(pair, carry):
        one = pl.ds(pl.multiple_of(pair * K_TILES, K_TILES), K_TILES)
        two = pl.ds(pl.multiple_of((pair + 16) * K_TILES, K_TILES), K_TILES)
        a1, a2 = total(0, one), total(0, two)
        b1, b2 = total(1, one), total(1, two)
        out_ref[one, :] = jnp.where(low_half, a1, b2) + pltpu.roll(jnp.where(low_half, a2, b1), 64, 1)
        return carry

    stores = []
    pairs = 16 // LOADS
    for i in range(LOADS):
        lax.fori_loop(i * pairs, (i + 1) * pairs, rows_of, 0, unroll=2)
        part = pl.ds(i * pairs * K_TILES, pairs * K_TILES)
        stores.append(pltpu.make_async_copy(out_ref.at[part, :], held_ref.at[part, :], store_sem.at[i]))
        stores[i].start()
    for store in stores:
        store.wait()


def row_tables():
    span = np.arange(K_TILES)
    c, s = waves(span, span, K_TILES)
    e = np.concatenate([c, s], 1)
    kx = np.arange(TILE)
    tc, ts = waves(kx, span, G)
    c32, s32 = waves(kx, kx, TILE)
    f = np.kron(np.eye(4), np.block([[c32, -s32], [s32, c32]]))
    return split_np(e) + (tc.astype(np.float32), ts.astype(np.float32)) + split_np(f)


TURNS = (2, 1, 3, 0)


def wait_for(ref, sem):
    pltpu.make_async_copy(ref, ref, sem).wait()


def send_to(source, target, send_sem, recv_sem, device):
    pltpu.make_async_remote_copy(
        src_ref=source,
        dst_ref=target,
        send_sem=send_sem,
        recv_sem=recv_sem,
        device_id=device,
        device_id_type=MESH,
    ).start()


def exchange_kernel(
    rows_ref, reh_ref, rel_ref, rtc_ref, rts_ref, rfh_ref, rfl_ref, eh_ref, el_ref, tc_ref, ts_ref,
    v_ref, held_ref, z_ref, out_ref, mid_ref, in_ref, load_sem, send_sem, mid_sem, recv_sem, own_sem,
):
    base, band = lax.axis_index("base"), lax.axis_index("band")
    my_x, my_y, my_core = base // 8, base // 2 % 4, base % 2
    loads = []
    for i in range(4):
        part = pl.ds(i * 4 * K_TILES, 4 * K_TILES)
        loads.append(pltpu.make_async_copy(rows_ref.at[part, :], held_ref.at[part, :], load_sem.at[i]))
        loads[i].start()
    barrier = pltpu.get_barrier_semaphore()
    for step in range(1, N_BAND):
        pl.semaphore_signal(barrier, inc=1, device_id=(base, (band + step) % N_BAND), device_id_type=MESH)
    for offset in OFFSETS:
        pl.semaphore_signal(barrier, inc=1, device_id=(moved(base, offset), band), device_id_type=MESH)

    quarter = lax.broadcasted_iota(jnp.int32, (8, 128), 1) // 32

    def transform(group):
        turned = [held_ref[pl.ds((4 * group + i) * K_TILES, K_TILES), :].T for i in range(4)]
        hh, hl = split(jnp.concatenate(turned, 0))
        prod = mm3(hh, hl, reh_ref[...], rel_ref[...])
        for i in range(2):
            parts = []
            for t in range(4):
                at = 256 * i + 64 * t
                re, im = prod[at : at + 32], prod[at + 32 : at + 64]
                y_re = re[:, 0:256] - im[:, 256:512]
                y_im = re[:, 256:512] + im[:, 0:256]
                parts.append(y_re * rtc_ref[...] - y_im * rts_ref[...])
                parts.append(y_re * rts_ref[...] + y_im * rtc_ref[...])
            vh, vl = split(jnp.concatenate(parts, 0))
            z = mm3(rfh_ref[...], rfl_ref[...], vh, vl)
            for half in range(2):
                for j in range(2):
                    at = pl.ds((4 * group + 2 * i + j) * Z_PITCH, 128)
                    z_ref[half, at, :] = z[128 * j : 128 * j + 128, 128 * half : 128 * half + 128]

    def blocks(part, to_y):
        def one(i, carry):
            x, core = i // 2, i % 2
            b2 = x * 8 + to_y * 2 + core
            for half in range(2):
                pieces = [z_ref[half, pl.ds(part * 8 * Z_PITCH + p * 32 + b2, 8, stride=Z_PITCH), :] for p in range(4)]
                for zq in range(4):
                    block = None
                    for p in range(4):
                        turned = pieces[p] if p == zq else pltpu.roll(pieces[p], (p - zq) * 32 % 128, 1)
                        block = turned if block is None else jnp.where(quarter == p, turned, block)
                    out_ref[x, to_y, core, half * 4 + zq, 8 * part : 8 * part + 8, :] = block
            return carry

        lax.fori_loop(0, 8, one, 0, unroll=4)

    def over_band(part, k):
        to_y = (my_y + TURNS[k]) % 4
        rows = pl.ds(8 * part, 8)
        blocks(part, to_y)
        if part + k == 0:
            pl.semaphore_wait(barrier, N_BAND - 1 + len(OFFSETS))
        groups = ((slice(None),),) if (part, k) != (1, 3) else (tuple((my_x + x) % 4 for x in (2, 1, 3)), (my_x,))
        for i, columns in enumerate(groups):
            sem = 4 * part + k + i
            for step in (4, 3, 5, 2, 6, 1, 7, 0):
                to = (band + step) % N_BAND
                for x in columns:
                    source = out_ref.at[x, to_y, :, to, rows, :]
                    target = mid_ref.at[x, to_y, :, band, rows, :]
                    if step:
                        send_to(source, target, send_sem, mid_sem.at[sem], (base, to))
                    else:
                        own_mid[sem].append(pltpu.make_async_copy(source, target, own_sem.at[len(started)]))
                        own_mid[sem][-1].start()
                        started.append(sem)

    def over_base(part, k, own_chip=None):
        to_y = (my_y + TURNS[k]) % 4
        rows = pl.ds(8 * part, 8)
        sem = 4 * part + k + int(bool(own_chip))
        for own in own_mid[sem]:
            own.wait()
        count = {None: 4, False: 3, True: 1}[own_chip]
        wait_for(out_ref.at[pl.ds(0, count), 0, :, pl.ds(0, N_BAND - 1), rows, :], mid_sem.at[sem])
        for x in {None: range(4), False: (2, 1, 3), True: (0,)}[own_chip]:
            for core in range(2):
                held = mid_ref.at[(my_x + x) % 4, to_y, (my_core + core) % 2, :, rows, :]
                target = in_ref.at[base, :, rows, :]
                if (x, TURNS[k], core) == (0, 0, 0):
                    own = pltpu.make_async_copy(held, target, own_sem.at[11 + part])
                    own.start()
                    own_in.append(own)
                else:
                    to = (moved(base, (x, TURNS[k], core)), band)
                    send_to(held, target, send_sem, recv_sem.at[sem], to)

    def first(k):
        for part in range(2):
            for i, count in enumerate(((8,), (7,), (6, 1))[0 if TURNS[k] else 1 + part]):
                came = in_ref.at[pl.ds(0, count), :, pl.ds(8 * part, 8), :]
                wait_for(came, recv_sem.at[4 * part + k + i])
            if TURNS[k] == 0:
                own_in[part].wait()
        from_y = (my_y - TURNS[k] + 4) % 4

        ids = [t // 2 * 8 + from_y * 2 + t % 2 for t in range(8)]
        lefts = []
        for j in ids:
            turned = in_ref[j].reshape(128, 128).T
            lefts.append(jnp.concatenate([turned[0:64], turned[64:128]], 1))
        dh, dl = split(jnp.concatenate(lefts, 0))
        prod = mm3(dh, dl, eh_ref[...], el_ref[...])
        for t, j in enumerate(ids):
            re, im = prod[64 * t : 64 * t + 32], prod[64 * t + 32 : 64 * t + 64]
            y_re = re[:, 0:256] - im[:, 256:512]
            y_im = re[:, 256:512] + im[:, 0:256]
            tc = tc_ref[pl.ds(j, 1), :]
            ts = ts_ref[pl.ds(j, 1), :]
            v_re = y_re * tc - y_im * ts
            v_im = y_re * ts + y_im * tc
            for half in range(2):
                lanes = slice(128 * half, 128 * half + 128)
                v_ref[half, pl.ds(j, 32, stride=PITCH), :] = v_re[:, lanes]
                v_ref[half, pl.ds(32 + j, 32, stride=PITCH), :] = v_im[:, lanes]

    own_mid, own_in, started = [[] for _ in range(9)], [], []
    for part in range(2):
        for i in range(2 * part, 2 * part + 2):
            loads[i].wait()
            transform(i)
        for k in range(4):
            over_band(part, k)
    for k in range(4):
        over_base(0, k)
    over_base(1, 0)
    over_base(1, 1)
    first(0)
    over_base(1, 2)
    first(1)
    over_base(1, 3, False)
    first(2)
    over_base(1, 3, True)
    first(3)
    wait_for(in_ref.at[pl.ds(0, 28)], send_sem)
    wait_for(in_ref.at[pl.ds(0, 31)], send_sem)


def column_kernel(v_ref, fh_ref, fl_ref, out_ref, x_ref):
    for i in range(8):
        rows = pl.ds(PITCH * i, 64)
        vh, vl = split(jnp.concatenate([v_ref[0, rows, :], v_ref[1, rows, :]], 1))
        x = mm3(fh_ref[...], fl_ref[...], vh, vl)
        for half in range(2):
            x_ref[half, rows, :] = x[:, 128 * half : 128 * half + 128]
    for c in range(2):
        for a2 in range(TILE):
            for half in range(2):
                at = a2 * 256 + half * 128
                out_ref[c, :, at : at + 128] = x_ref[half, pl.ds(c * 32 + a2, 8, stride=PITCH), :]


def column_tables():
    zs, rp, rpp = np.arange(8), np.arange(16), np.arange(2)
    r = (rpp[:, None, None] * 16 + zs[None, :, None] * 32 + rp[None, None, :]).reshape(-1)
    span = np.arange(K_TILES)
    c, s = waves(r, span, K_TILES)
    e = np.concatenate([c, s], 1)
    ky = np.arange(TILE)
    tc, ts = waves(ky, span, G)
    c32, s32 = waves(ky, ky, TILE)
    f = np.block([[c32, -s32], [s32, c32]]) / G
    return split_np(e) + (tc.astype(np.float32), ts.astype(np.float32)) + split_np(f)


VMEM = pl.BlockSpec(memory_space=pltpu.VMEM)
HBM = pl.BlockSpec(memory_space=pl.ANY)
LIMIT = pltpu.CompilerParams(vmem_limit_bytes=56 * 2**20)


def shards(visibilities, coords, chan_scale, taper_gain, owner_base, tile_cell):
    arrived, ids = pl.pallas_call(
        grid_kernel,
        out_shape=(
            jax.ShapeDtypeStruct((N_BASE, PAIRS, 128), F32),
            jax.ShapeDtypeStruct((N_BASE, 2, PAIRS), jnp.int32),
        ),
        in_specs=[VMEM] * 13,
        out_specs=(HBM, HBM),
        scratch_shapes=[
            pltpu.VMEM((2, 4, SLOT, 128), F32),
            pltpu.VMEM((TILE * ROWS, 128), F32),
            pltpu.VMEM((2, PAIRS), jnp.int32),
            pltpu.VMEM((2, SLOT, 128), F32),
            pltpu.VMEM((TILE, 128), F32),
            pltpu.SemaphoreType.DMA((2,)),
            pltpu.SemaphoreType.DMA((2,)),
            pltpu.SemaphoreType.DMA((2,)),
        ],
        compiler_params=pltpu.CompilerParams(vmem_limit_bytes=56 * 2**20, collective_id=0, has_side_effects=True),
        name="gridding",
    )(
        visibilities,
        coords.transpose(1, 2, 0),
        chan_scale.reshape(1, 16),
        owner_base.reshape(2, PAIRS),
        tile_cell.reshape(2, PAIRS),
        taper_gain,
        *[jnp.asarray(t) for t in grid_tables()],
    )
    tables = [jnp.asarray(t) for t in column_tables()]
    row_side = [jnp.asarray(t) for t in row_tables()]
    rows = pl.pallas_call(
        row_kernel,
        out_shape=jax.ShapeDtypeStruct((G // 2, 128), F32),
        in_specs=[HBM, HBM],
        out_specs=HBM,
        scratch_shapes=[
            pltpu.VMEM((N_BASE, PAIRS, 128), F32),
            pltpu.VMEM((G // 2, 128), F32),
            pltpu.SMEM((N_BASE, 2, PAIRS), jnp.int32),
            pltpu.SemaphoreType.DMA((LOADS,)),
            pltpu.SemaphoreType.DMA((LOADS,)),
            pltpu.SemaphoreType.DMA,
            *[pltpu.VMEM((G, 128), F32)] * CHAINS,
        ],
        compiler_params=LIMIT,
        name="rows",
    )(arrived, ids)
    by_target = pltpu.VMEM((4, 4, 2, N_BAND, 16, 128), F32)
    dma = pltpu.SemaphoreType.DMA
    turned = pl.pallas_call(
        exchange_kernel,
        out_shape=jax.ShapeDtypeStruct((2, TILE * PITCH, 128), F32),
        in_specs=[HBM] + [VMEM] * 10,
        out_specs=VMEM,
        scratch_shapes=[
            pltpu.VMEM((G // 2, 128), F32),
            pltpu.VMEM((2, 16 * Z_PITCH, 128), F32),
            by_target,
            by_target,
            pltpu.VMEM((N_BASE, N_BAND, 16, 128), F32),
            dma((4,)),
            dma,
            dma((9,)),
            dma((9,)),
            dma((13,)),
        ],
        compiler_params=pltpu.CompilerParams(vmem_limit_bytes=56 * 2**20, collective_id=1, has_side_effects=True),
        name="exchange",
    )(rows, *row_side, *tables[:4])
    return pl.pallas_call(
        column_kernel,
        out_shape=jax.ShapeDtypeStruct((2, TILE, G), F32),
        grid=(TILE // 8,),
        in_specs=[
            pl.BlockSpec((2, 8 * PITCH, 128), lambda i: (0, i, 0)),
            pl.BlockSpec((64, 64), lambda i: (0, 0)),
            pl.BlockSpec((64, 64), lambda i: (0, 0)),
        ],
        out_specs=pl.BlockSpec((2, 8, G), lambda i: (0, i, 0)),
        scratch_shapes=[pltpu.VMEM((2, 8 * PITCH, 128), F32)],
        compiler_params=LIMIT,
        name="columns",
    )(turned, *tables[4:])


def solution(mesh):
    placed = (
        P(("base", "band"), None, None),
        P(("base", "band"), None, None),
        P(),
        P(),
        P(("base", "band"), None),
        P(("base", "band")),
    )
    return jax.shard_map(
        shards,
        mesh=mesh,
        in_specs=placed,
        out_specs=P(None, ("base", "band"), None),
        check_vma=False,
    )
```

```python
import functools
import math

import jax
import jax.numpy as jnp
import ml_dtypes
import numpy as np
from jax import lax
from jax.experimental import pallas as pl
from jax.experimental.pallas import tpu as pltpu
from jax.sharding import PartitionSpec as P

G = 8192
TILE = 32
SLOT = 256
PAIRS = SLOT // 2
N_BASE = 32
N_BAND = 8
K_TILES = G // TILE
ROWS = PAIRS + 8
F32 = jnp.float32
BF16 = jnp.bfloat16


def split_np(table):
    table = np.asarray(table, np.float64)
    high = table.astype(np.float32).astype(ml_dtypes.bfloat16)
    low = (table - high.astype(np.float64)).astype(np.float32).astype(ml_dtypes.bfloat16)
    return high, low


def waves(first, second, length):
    turns = np.outer(np.asarray(first), np.asarray(second)) % length
    angle = 2.0 * np.pi / length * turns
    return np.cos(angle), np.sin(angle)


def split(x):
    high = x.astype(BF16)
    low = (x - high.astype(F32)).astype(BF16)
    return high, low


def mm(a, b):
    return lax.dot_general(a, b, (((1,), (0,)), ((), ())), preferred_element_type=F32)


def mm_nt(a, b):
    return lax.dot_general(a, b, (((1,), (1,)), ((), ())), preferred_element_type=F32)


def mm3(ah, al, bh, bl):
    rows = ah.shape[0]
    both = mm(jnp.concatenate([ah, al], 0), bh)
    return both[:rows] + (both[rows:] + mm(ah, bl))


def fit_waves():
    r = 0.5 * np.cos(np.pi * (np.arange(4000) + 0.5) / 4000)
    odd = np.stack([r ** (2 * i + 1) for i in range(7)], 1)
    even = np.stack([r ** (2 * i) for i in range(8)], 1)
    s = np.linalg.lstsq(odd, np.sin(2 * np.pi * r), rcond=None)[0]
    c = np.linalg.lstsq(even, np.cos(2 * np.pi * r), rcond=None)[0]
    return [float(np.float32(v)) for v in s], [float(np.float32(v)) for v in c]


SIN_C, COS_C = fit_waves()


def cos_sin_turns(turns):
    r = turns - jnp.floor(turns + 0.5)
    r2 = r * r
    s = jnp.full_like(r, SIN_C[-1])
    for v in SIN_C[-2::-1]:
        s = s * r2 + v
    c = jnp.full_like(r, COS_C[-1])
    for v in COS_C[-2::-1]:
        c = c * r2 + v
    return c, s * r


UNIT = 32
SENDS = 8
MESH = pl.DeviceIdType.MESH
OFFSETS = sorted(
    [(x, y, c) for x in range(4) for y in range(4) for c in range(2) if (x, y, c) != (0, 0, 0)],
    key=lambda d: ((d[0] + d[1]) % 4, d[0], d[2]),
)


def moved(base, offset):
    x, y, c = base // 8, base // 2 % 4, base % 2
    return (x + offset[0]) % 4 * 8 + (y + offset[1]) % 4 * 2 + (c + offset[2]) % 2
PITCH = 72
Z_PITCH = 136
CHAINS = 8
LOADS = 4


def powers(base, w8, w16):
    c, s = base
    c8, s8 = w8
    c16, s16 = w16
    return [
        (c * c16 + s * s16, s * c16 - c * s16),
        (c * c8 + s * s8, s * c8 - c * s8),
        (c, s),
        (c * c8 - s * s8, s * c8 + c * s8),
    ]


def spread(values, table):
    high = values.astype(BF16)
    rest = values - high.astype(F32)
    mid = rest.astype(BF16)
    low = (rest - mid.astype(F32)).astype(BF16)
    return mm(high, table) + mm(mid, table) + mm(low, table)


def grid_kernel(
    vis_ref, coords_ref, chan_ref, owner_ref, cell_ref, taper_in_ref, time_ref, chan_at_ref, tile_at_ref,
    kxh_ref, kxl_ref, fyh_ref, fyl_ref,
    all_ref, all_ids_ref, w_ref, out_ref, ids_ref, places_ref, taper_ref, send_sem, recv_sem, own_sem,
):
    base, band = lax.axis_index("base"), lax.axis_index("band")
    barrier = pltpu.get_barrier_semaphore()
    for offset in OFFSETS:
        pl.semaphore_signal(barrier, inc=1, device_id=(moved(base, offset), band), device_id_type=MESH)
    step8 = lax.broadcasted_iota(jnp.int32, (8, 128), 0).astype(F32)
    lane = lax.broadcasted_iota(jnp.int32, (32, 128), 1)
    taper_ref[...] = spread(taper_in_ref[...], tile_at_ref[...])
    scale = spread(jnp.broadcast_to(chan_ref[...], (8, 16)), chan_at_ref[...])[0:1] * (1.0 / TILE)
    cell = cell_ref[...]
    ids_ref[...] = (cell >> 3) * K_TILES + owner_ref[...] * 8 + (cell & 7)
    for side in range(2):
        places_ref[side] = spread(coords_ref[side].T, time_ref[...]) * scale
    def one(s):
        def phases(side):
            row = pl.ds(s, 1)
            turns = places_ref[side, row, :] * step8
            w = [jnp.broadcast_to(w_ref[side, i, row, :], (8, 128)) for i in range(4)]
            return powers(cos_sin_turns(turns), (w[0], w[1]), (w[2], w[3]))

        x_side = phases(0)
        y_side = phases(1)
        vr = jnp.broadcast_to(vis_ref[s, 0:1, :], (8, 128))
        vi = jnp.broadcast_to(vis_ref[s, 1:2, :], (8, 128))
        l_re = jnp.concatenate([vr * c - vi * s for c, s in y_side], 0)
        l_im = jnp.concatenate([vr * s + vi * c for c, s in y_side], 0)
        c_x = jnp.concatenate([c for c, s in x_side], 0)
        s_x = jnp.concatenate([s for c, s in x_side], 0)
        lrh, lrl = split(l_re)
        lih, lil = split(l_im)
        ch, cl = split(c_x)
        sh, sl = split(s_x)
        left = jnp.concatenate([jnp.concatenate([lrh, lih], 1), jnp.concatenate([lrl, lil], 1)], 0)
        right_h = jnp.concatenate([jnp.concatenate([ch, -sh], 1), jnp.concatenate([sh, ch], 1)], 0)
        right_l = jnp.concatenate([jnp.concatenate([cl, -sl], 1), jnp.concatenate([sl, cl], 1)], 0)
        return left, right_h, right_l

    def body(step, carry):
        first = step * (UNIT // 2)
        for half in range(2):
            rows = pl.ds(pl.multiple_of(half * PAIRS + first, UNIT // 2), UNIT // 2)
            for side in range(2):
                c8, s8 = cos_sin_turns(places_ref[side, rows, :] * 8.0)
                w_ref[side, 0, rows, :] = c8
                w_ref[side, 1, rows, :] = s8
                w_ref[side, 2, rows, :] = c8 * c8 - s8 * s8
                w_ref[side, 3, rows, :] = 2.0 * (c8 * s8)
        pixels = []
        for pair in range(UNIT // 2):
            a, b = one(first + pair), one(PAIRS + first + pair)
            left_h = jnp.concatenate([a[0][0:32], b[0][0:32]], 0)
            left_l = jnp.concatenate([a[0][32:64], b[0][32:64]], 0)
            right_h = jnp.concatenate([a[1], b[1]], 0)
            right_l = jnp.concatenate([a[2], b[2]], 0)
            both = mm_nt(jnp.concatenate([left_h, left_l], 0), right_h)
            prod = both[0:64] + (both[64:128] + mm_nt(left_h, right_l))
            pixels.append(jnp.where(lane < 64, prod[0:32], prod[32:64]) * taper_ref[...])
        ph, pl_ = split(jnp.concatenate(pixels, 0))
        q = mm3(ph, pl_, kxh_ref[...], kxl_ref[...])
        for pair in range(UNIT // 2):
            rows = slice(pair * 32, pair * 32 + 32)
            col = jnp.concatenate([q[rows, 0:128], q[rows, 128:256]], 0)
            qh, ql = split(col)
            tile = mm3(fyh_ref[...], fyl_ref[...], qh, ql)
            out_ref[pl.ds(first + pair, 32, stride=ROWS), :] = tile
        return carry

    steps = SLOT // UNIT // SENDS

    def send(part, rows):
        for offset in OFFSETS:
            to = moved(base, offset)
            pltpu.make_async_remote_copy(
                src_ref=out_ref.at[pl.ds(pl.multiple_of(to * ROWS + part, 8), rows), :],
                dst_ref=all_ref.at[base, pl.ds(pl.multiple_of(part, 8), rows), :],
                send_sem=send_sem.at[0],
                recv_sem=recv_sem.at[0],
                device_id=(to, band),
                device_id_type=MESH,
            ).start()

    rows = PAIRS // SENDS
    lax.fori_loop(0, steps, body, 0)
    pl.semaphore_wait(barrier, len(OFFSETS))
    send(0, rows)
    for offset in OFFSETS:
        pltpu.make_async_remote_copy(
            src_ref=ids_ref,
            dst_ref=all_ids_ref.at[base],
            send_sem=send_sem.at[1],
            recv_sem=recv_sem.at[1],
            device_id=(moved(base, offset), band),
            device_id_type=MESH,
        ).start()

    def later(part, carry):
        lax.fori_loop(part * steps, part * steps + steps, body, 0)
        send(part * rows, rows)
        return carry

    lax.fori_loop(1, SENDS - 1, later, 0)
    lax.fori_loop(SLOT // UNIT - steps, SLOT // UNIT, body, 0)
    send(PAIRS - rows, rows)
    own = [
        pltpu.make_async_copy(
            out_ref.at[pl.ds(pl.multiple_of(base * ROWS, 8), PAIRS), :], all_ref.at[base], own_sem.at[0]
        ),
        pltpu.make_async_copy(ids_ref, all_ids_ref.at[base], own_sem.at[1]),
    ]
    for copy in own:
        copy.start()
    for copy in own:
        copy.wait()
    for i, ref in enumerate((all_ref, all_ids_ref)):
        arrived = ref.at[pl.ds(0, len(OFFSETS))]
        pltpu.make_async_copy(arrived, arrived, send_sem.at[i]).wait()
        pltpu.make_async_copy(arrived, arrived, recv_sem.at[i]).wait()


def grid_tables():
    span = np.arange(TILE)
    c, s = waves(span, span, TILE)
    eye2 = np.eye(2)
    fx = np.block([[c, -s], [s, c]])
    fx_turned = np.block([[-s, -c], [c, -s]])
    kx = np.concatenate([np.kron(eye2, fx), np.kron(eye2, fx_turned)], 1)
    fy = np.concatenate([c, s], 1) / (TILE * math.sqrt(128.0))
    q = np.arange(128)
    time_at = np.equal.outer(np.arange(8), q // 16)
    chan_at = np.equal.outer(np.arange(16), q % 16)
    tile_at = np.equal.outer(span, q % TILE)
    ones = tuple(t.astype(np.float32).astype(ml_dtypes.bfloat16) for t in (time_at, chan_at, tile_at))
    return ones + split_np(kx) + split_np(fy)


def row_kernel(all_ref, all_ids_ref, held_ref, in_ref, out_ref, ids_ref, load_sem, store_sem, ids_sem, *accs):
    ids_copy = pltpu.make_async_copy(all_ids_ref, ids_ref, ids_sem)
    ids_copy.start()
    sources = N_BASE // LOADS
    loads = []
    for i in range(LOADS):
        part = pl.ds(i * sources, sources)
        loads.append(
            pltpu.make_async_copy(all_ref.at[part], in_ref.at[part], load_sem.at[i])
        )
        loads[i].start()
    def clear(i, carry):
        rows = pl.ds(pl.multiple_of(i * 64, 64), 64)
        for acc in accs:
            acc[rows, :] = jnp.zeros((64, 128), F32)
        return carry

    lax.fori_loop(0, G // 64, clear, 0)
    ids_copy.wait()

    def add(src, carry):
        for t in range(PAIRS):
            row = in_ref[src, t : t + 1, :]
            for half in range(2):
                acc = accs[(2 * t + half) % CHAINS]
                at = pl.ds(ids_ref[src, half, t], 1)
                acc[at, :] = acc[at, :] + row
        return carry

    for i in range(LOADS):
        loads[i].wait()
        lax.fori_loop(i * sources, (i + 1) * sources, add, 0)

    def total(half, rows):
        parts = [acc[rows, :] for acc in accs[half::2]]
        while len(parts) > 1:
            parts = [x + y for x, y in zip(parts[::2], parts[1::2])]
        return parts[0]

    low_half = lax.broadcasted_iota(jnp.int32, (K_TILES, 128), 1) < 64

    def rows_of(pair, carry):
        one = pl.ds(pl.multiple_of(pair * K_TILES, K_TILES), K_TILES)
        two = pl.ds(pl.multiple_of((pair + 16) * K_TILES, K_TILES), K_TILES)
        a1, a2 = total(0, one), total(0, two)
        b1, b2 = total(1, one), total(1, two)
        out_ref[one, :] = jnp.where(low_half, a1, b2) + pltpu.roll(jnp.where(low_half, a2, b1), 64, 1)
        return carry

    stores = []
    pairs = 16 // LOADS
    for i in range(LOADS):
        lax.fori_loop(i * pairs, (i + 1) * pairs, rows_of, 0, unroll=2)
        part = pl.ds(i * pairs * K_TILES, pairs * K_TILES)
        stores.append(pltpu.make_async_copy(out_ref.at[part, :], held_ref.at[part, :], store_sem.at[i]))
        stores[i].start()
    for store in stores:
        store.wait()


def row_tables():
    span = np.arange(K_TILES)
    c, s = waves(span, span, K_TILES)
    e = np.concatenate([c, s], 1)
    kx = np.arange(TILE)
    tc, ts = waves(kx, span, G)
    c32, s32 = waves(kx, kx, TILE)
    f = np.kron(np.eye(4), np.block([[c32, -s32], [s32, c32]]))
    return split_np(e) + (tc.astype(np.float32), ts.astype(np.float32)) + split_np(f)


TURNS = (2, 1, 3, 0)
FAR = (2, 1, 3)


def wait_for(ref, sem):
    pltpu.make_async_copy(ref, ref, sem).wait()


def send_to(source, target, send_sem, recv_sem, device):
    pltpu.make_async_remote_copy(
        src_ref=source,
        dst_ref=target,
        send_sem=send_sem,
        recv_sem=recv_sem,
        device_id=device,
        device_id_type=MESH,
    ).start()


def exchange_kernel(
    rows_ref, reh_ref, rel_ref, rtc_ref, rts_ref, rfh_ref, rfl_ref, eh_ref, el_ref, tc_ref, ts_ref,
    v_ref, held_ref, z_ref, out_ref, mid_ref, in_ref, load_sem, send_sem, mid_sem, recv_sem, own_sem,
):
    base, band = lax.axis_index("base"), lax.axis_index("band")
    my_x, my_y, my_core = base // 8, base // 2 % 4, base % 2
    loads = []
    for i in range(4):
        part = pl.ds(i * 4 * K_TILES, 4 * K_TILES)
        loads.append(pltpu.make_async_copy(rows_ref.at[part, :], held_ref.at[part, :], load_sem.at[i]))
        loads[i].start()
    barrier = pltpu.get_barrier_semaphore()
    for step in range(1, N_BAND):
        pl.semaphore_signal(barrier, inc=1, device_id=(base, (band + step) % N_BAND), device_id_type=MESH)
    for offset in OFFSETS:
        pl.semaphore_signal(barrier, inc=1, device_id=(moved(base, offset), band), device_id_type=MESH)

    quarter = lax.broadcasted_iota(jnp.int32, (8, 128), 1) // 32

    def transform(group):
        turned = [held_ref[pl.ds((4 * group + i) * K_TILES, K_TILES), :].T for i in range(4)]
        hh, hl = split(jnp.concatenate(turned, 0))
        prod = mm3(hh, hl, reh_ref[...], rel_ref[...])
        for i in range(2):
            parts = []
            for t in range(4):
                at = 256 * i + 64 * t
                re, im = prod[at : at + 32], prod[at + 32 : at + 64]
                y_re = re[:, 0:256] - im[:, 256:512]
                y_im = re[:, 256:512] + im[:, 0:256]
                parts.append(y_re * rtc_ref[...] - y_im * rts_ref[...])
                parts.append(y_re * rts_ref[...] + y_im * rtc_ref[...])
            vh, vl = split(jnp.concatenate(parts, 0))
            z = mm3(rfh_ref[...], rfl_ref[...], vh, vl)
            for half in range(2):
                for j in range(2):
                    at = pl.ds((4 * group + 2 * i + j) * Z_PITCH, 128)
                    z_ref[half, at, :] = z[128 * j : 128 * j + 128, 128 * half : 128 * half + 128]

    def blocks(part, to_y):
        def one(i, carry):
            x, core = i // 2, i % 2
            b2 = x * 8 + to_y * 2 + core
            for half in range(2):
                pieces = [z_ref[half, pl.ds(part * 8 * Z_PITCH + p * 32 + b2, 8, stride=Z_PITCH), :] for p in range(4)]
                for zq in range(4):
                    block = None
                    for p in range(4):
                        turned = pieces[p] if p == zq else pltpu.roll(pieces[p], (p - zq) * 32 % 128, 1)
                        block = turned if block is None else jnp.where(quarter == p, turned, block)
                    out_ref[x, to_y, core, half * 4 + zq, 8 * part : 8 * part + 8, :] = block
            return carry

        lax.fori_loop(0, 8, one, 0, unroll=4)

    def over_band(part, k):
        to_y = (my_y + TURNS[k]) % 4
        rows = pl.ds(8 * part, 8)
        blocks(part, to_y)
        if part + k == 0:
            pl.semaphore_wait(barrier, N_BAND - 1 + len(OFFSETS))
        if k < 3:
            band_copies(4 * part + k, (slice(None),), to_y, rows)
        else:
            band_copies(4 * part + k, [(my_x + x) % 4 for x in FAR], to_y, rows)
        if (part, k) == (1, 3):
            band_copies(8, (my_x,), to_y, pl.ds(0, 16))

    def band_copies(sem, columns, to_y, rows):
        for step in (4, 3, 5, 2, 6, 1, 7, 0):
            to = (band + step) % N_BAND
            for x in columns:
                source = out_ref.at[x, to_y, :, to, rows, :]
                target = mid_ref.at[x, to_y, :, band, rows, :]
                if step:
                    send_to(source, target, send_sem, mid_sem.at[sem], (base, to))
                else:
                    own_mid[sem].append(pltpu.make_async_copy(source, target, own_sem.at[len(started)]))
                    own_mid[sem][-1].start()
                    started.append(sem)

    def over_base(part, k):
        rows = pl.ds(8 * part, 8) if part < 2 else pl.ds(0, 16)
        sem = 4 * part + k if part < 2 else 8
        offsets = (0,) if part == 2 else range(4) if k < 3 else FAR
        to_y = (my_y + TURNS[k]) % 4
        for own in own_mid[sem]:
            own.wait()
        wait_for(out_ref.at[pl.ds(0, len(offsets)), 0, :, pl.ds(0, N_BAND - 1), rows, :], mid_sem.at[sem])
        for x in offsets:
            for core in range(2):
                held = mid_ref.at[(my_x + x) % 4, to_y, (my_core + core) % 2, :, rows, :]
                target = in_ref.at[base, :, rows, :]
                if (x, TURNS[k], core) == (0, 0, 0):
                    own = pltpu.make_async_copy(held, target, own_sem.at[13])
                    own.start()
                    own_in.append(own)
                else:
                    to = (moved(base, (x, TURNS[k], core)), band)
                    send_to(held, target, send_sem, recv_sem.at[sem], to)

    def first(k):
        for part in range(2):
            wait_for(in_ref.at[pl.ds(0, 8 if k < 3 else 6), :, pl.ds(8 * part, 8), :], recv_sem.at[4 * part + k])
        if k == 3:
            wait_for(in_ref.at[0], recv_sem.at[8])
            own_in[0].wait()
        from_y = (my_y - TURNS[k] + 4) % 4

        ids = [t // 2 * 8 + from_y * 2 + t % 2 for t in range(8)]
        lefts = []
        for j in ids:
            turned = in_ref[j].reshape(128, 128).T
            lefts.append(jnp.concatenate([turned[0:64], turned[64:128]], 1))
        dh, dl = split(jnp.concatenate(lefts, 0))
        prod = mm3(dh, dl, eh_ref[...], el_ref[...])
        for t, j in enumerate(ids):
            re, im = prod[64 * t : 64 * t + 32], prod[64 * t + 32 : 64 * t + 64]
            y_re = re[:, 0:256] - im[:, 256:512]
            y_im = re[:, 256:512] + im[:, 0:256]
            tc = tc_ref[pl.ds(j, 1), :]
            ts = ts_ref[pl.ds(j, 1), :]
            v_re = y_re * tc - y_im * ts
            v_im = y_re * ts + y_im * tc
            for half in range(2):
                lanes = slice(128 * half, 128 * half + 128)
                v_ref[half, pl.ds(j, 32, stride=PITCH), :] = v_re[:, lanes]
                v_ref[half, pl.ds(32 + j, 32, stride=PITCH), :] = v_im[:, lanes]

    own_mid, own_in, started = [[] for _ in range(9)], [], []
    for part in range(2):
        for i in range(2 * part, 2 * part + 2):
            loads[i].wait()
            transform(i)
        for k in range(4):
            over_band(part, k)
    for k in range(4):
        over_base(0, k)
    over_base(1, 0)
    over_base(1, 1)
    first(0)
    over_base(1, 2)
    first(1)
    over_base(1, 3)
    first(2)
    over_base(2, 3)
    first(3)
    wait_for(in_ref.at[pl.ds(0, 28)], send_sem)
    wait_for(in_ref.at[pl.ds(0, 31)], send_sem)


def column_kernel(v_ref, fh_ref, fl_ref, out_ref, x_ref):
    for i in range(8):
        rows = pl.ds(PITCH * i, 64)
        vh, vl = split(jnp.concatenate([v_ref[0, rows, :], v_ref[1, rows, :]], 1))
        x = mm3(fh_ref[...], fl_ref[...], vh, vl)
        for half in range(2):
            x_ref[half, rows, :] = x[:, 128 * half : 128 * half + 128]
    for c in range(2):
        for a2 in range(TILE):
            for half in range(2):
                at = a2 * 256 + half * 128
                out_ref[c, :, at : at + 128] = x_ref[half, pl.ds(c * 32 + a2, 8, stride=PITCH), :]


def column_tables():
    zs, rp, rpp = np.arange(8), np.arange(16), np.arange(2)
    r = (rpp[:, None, None] * 16 + zs[None, :, None] * 32 + rp[None, None, :]).reshape(-1)
    span = np.arange(K_TILES)
    c, s = waves(r, span, K_TILES)
    e = np.concatenate([c, s], 1)
    ky = np.arange(TILE)
    tc, ts = waves(ky, span, G)
    c32, s32 = waves(ky, ky, TILE)
    f = np.block([[c32, -s32], [s32, c32]]) / G
    return split_np(e) + (tc.astype(np.float32), ts.astype(np.float32)) + split_np(f)


VMEM = pl.BlockSpec(memory_space=pltpu.VMEM)
HBM = pl.BlockSpec(memory_space=pl.ANY)
LIMIT = pltpu.CompilerParams(vmem_limit_bytes=56 * 2**20)


def shards(visibilities, coords, chan_scale, taper_gain, owner_base, tile_cell):
    arrived, ids = pl.pallas_call(
        grid_kernel,
        out_shape=(
            jax.ShapeDtypeStruct((N_BASE, PAIRS, 128), F32),
            jax.ShapeDtypeStruct((N_BASE, 2, PAIRS), jnp.int32),
        ),
        in_specs=[VMEM] * 13,
        out_specs=(HBM, HBM),
        scratch_shapes=[
            pltpu.VMEM((2, 4, SLOT, 128), F32),
            pltpu.VMEM((TILE * ROWS, 128), F32),
            pltpu.VMEM((2, PAIRS), jnp.int32),
            pltpu.VMEM((2, SLOT, 128), F32),
            pltpu.VMEM((TILE, 128), F32),
            pltpu.SemaphoreType.DMA((2,)),
            pltpu.SemaphoreType.DMA((2,)),
            pltpu.SemaphoreType.DMA((2,)),
        ],
        compiler_params=pltpu.CompilerParams(vmem_limit_bytes=56 * 2**20, collective_id=0, has_side_effects=True),
        name="gridding",
    )(
        visibilities,
        coords.transpose(1, 2, 0),
        chan_scale.reshape(1, 16),
        owner_base.reshape(2, PAIRS),
        tile_cell.reshape(2, PAIRS),
        taper_gain,
        *[jnp.asarray(t) for t in grid_tables()],
    )
    tables = [jnp.asarray(t) for t in column_tables()]
    row_side = [jnp.asarray(t) for t in row_tables()]
    rows = pl.pallas_call(
        row_kernel,
        out_shape=jax.ShapeDtypeStruct((G // 2, 128), F32),
        in_specs=[HBM, HBM],
        out_specs=HBM,
        scratch_shapes=[
            pltpu.VMEM((N_BASE, PAIRS, 128), F32),
            pltpu.VMEM((G // 2, 128), F32),
            pltpu.SMEM((N_BASE, 2, PAIRS), jnp.int32),
            pltpu.SemaphoreType.DMA((LOADS,)),
            pltpu.SemaphoreType.DMA((LOADS,)),
            pltpu.SemaphoreType.DMA,
            *[pltpu.VMEM((G, 128), F32)] * CHAINS,
        ],
        compiler_params=LIMIT,
        name="rows",
    )(arrived, ids)
    by_target = pltpu.VMEM((4, 4, 2, N_BAND, 16, 128), F32)
    dma = pltpu.SemaphoreType.DMA
    turned = pl.pallas_call(
        exchange_kernel,
        out_shape=jax.ShapeDtypeStruct((2, TILE * PITCH, 128), F32),
        in_specs=[HBM] + [VMEM] * 10,
        out_specs=VMEM,
        scratch_shapes=[
            pltpu.VMEM((G // 2, 128), F32),
            pltpu.VMEM((2, 16 * Z_PITCH, 128), F32),
            by_target,
            by_target,
            pltpu.VMEM((N_BASE, N_BAND, 16, 128), F32),
            dma((4,)),
            dma,
            dma((9,)),
            dma((9,)),
            dma((14,)),
        ],
        compiler_params=pltpu.CompilerParams(vmem_limit_bytes=56 * 2**20, collective_id=1, has_side_effects=True),
        name="exchange",
    )(rows, *row_side, *tables[:4])
    return pl.pallas_call(
        column_kernel,
        out_shape=jax.ShapeDtypeStruct((2, TILE, G), F32),
        grid=(TILE // 8,),
        in_specs=[
            pl.BlockSpec((2, 8 * PITCH, 128), lambda i: (0, i, 0)),
            pl.BlockSpec((64, 64), lambda i: (0, 0)),
            pl.BlockSpec((64, 64), lambda i: (0, 0)),
        ],
        out_specs=pl.BlockSpec((2, 8, G), lambda i: (0, i, 0)),
        scratch_shapes=[pltpu.VMEM((2, 8 * PITCH, 128), F32)],
        compiler_params=LIMIT,
        name="columns",
    )(turned, *tables[4:])


def solution(mesh):
    placed = (
        P(("base", "band"), None, None),
        P(("base", "band"), None, None),
        P(),
        P(),
        P(("base", "band"), None),
        P(("base", "band")),
    )
    return jax.shard_map(
        shards,
        mesh=mesh,
        in_specs=placed,
        out_specs=P(None, ("base", "band"), None),
        check_vma=False,
    )
```

```python
import functools
import math

import jax
import jax.numpy as jnp
import ml_dtypes
import numpy as np
from jax import lax
from jax.experimental import pallas as pl
from jax.experimental.pallas import tpu as pltpu
from jax.sharding import PartitionSpec as P

G = 8192
TILE = 32
SLOT = 256
PAIRS = SLOT // 2
N_BASE = 32
N_BAND = 8
K_TILES = G // TILE
ROWS = PAIRS + 8
F32 = jnp.float32
BF16 = jnp.bfloat16


def split_np(table):
    table = np.asarray(table, np.float64)
    high = table.astype(np.float32).astype(ml_dtypes.bfloat16)
    low = (table - high.astype(np.float64)).astype(np.float32).astype(ml_dtypes.bfloat16)
    return high, low


def waves(first, second, length):
    turns = np.outer(np.asarray(first), np.asarray(second)) % length
    angle = 2.0 * np.pi / length * turns
    return np.cos(angle), np.sin(angle)


def split(x):
    high = x.astype(BF16)
    low = (x - high.astype(F32)).astype(BF16)
    return high, low


def mm(a, b):
    return lax.dot_general(a, b, (((1,), (0,)), ((), ())), preferred_element_type=F32)


def mm_nt(a, b):
    return lax.dot_general(a, b, (((1,), (1,)), ((), ())), preferred_element_type=F32)


def mm3(ah, al, bh, bl):
    rows = ah.shape[0]
    both = mm(jnp.concatenate([ah, al], 0), bh)
    return both[:rows] + (both[rows:] + mm(ah, bl))


def fit_waves():
    r = 0.5 * np.cos(np.pi * (np.arange(4000) + 0.5) / 4000)
    odd = np.stack([r ** (2 * i + 1) for i in range(7)], 1)
    even = np.stack([r ** (2 * i) for i in range(8)], 1)
    s = np.linalg.lstsq(odd, np.sin(2 * np.pi * r), rcond=None)[0]
    c = np.linalg.lstsq(even, np.cos(2 * np.pi * r), rcond=None)[0]
    return [float(np.float32(v)) for v in s], [float(np.float32(v)) for v in c]


SIN_C, COS_C = fit_waves()


def cos_sin_turns(turns):
    r = turns - jnp.floor(turns + 0.5)
    r2 = r * r
    s = jnp.full_like(r, SIN_C[-1])
    for v in SIN_C[-2::-1]:
        s = s * r2 + v
    c = jnp.full_like(r, COS_C[-1])
    for v in COS_C[-2::-1]:
        c = c * r2 + v
    return c, s * r


UNIT = 32
SENDS = 8
MESH = pl.DeviceIdType.MESH
OFFSETS = sorted(
    [(x, y, c) for x in range(4) for y in range(4) for c in range(2) if (x, y, c) != (0, 0, 0)],
    key=lambda d: ((d[0] + d[1]) % 4, d[0], d[2]),
)


def moved(base, offset):
    x, y, c = base // 8, base // 2 % 4, base % 2
    return (x + offset[0]) % 4 * 8 + (y + offset[1]) % 4 * 2 + (c + offset[2]) % 2
PITCH = 72
Z_PITCH = 136
CHAINS = 8
LOADS = 4


def powers(base, w8, w16):
    c, s = base
    c8, s8 = w8
    c16, s16 = w16
    return [
        (c * c16 + s * s16, s * c16 - c * s16),
        (c * c8 + s * s8, s * c8 - c * s8),
        (c, s),
        (c * c8 - s * s8, s * c8 + c * s8),
    ]


def spread(values, table):
    high = values.astype(BF16)
    rest = values - high.astype(F32)
    mid = rest.astype(BF16)
    low = (rest - mid.astype(F32)).astype(BF16)
    return mm(high, table) + mm(mid, table) + mm(low, table)


def grid_kernel(
    vis_ref, coords_ref, chan_ref, owner_ref, cell_ref, taper_in_ref, time_ref, chan_at_ref, tile_at_ref,
    kxh_ref, kxl_ref, fyh_ref, fyl_ref,
    all_ref, all_ids_ref, w_ref, out_ref, ids_ref, places_ref, taper_ref, send_sem, recv_sem, own_sem,
):
    base, band = lax.axis_index("base"), lax.axis_index("band")
    barrier = pltpu.get_barrier_semaphore()
    for offset in OFFSETS:
        pl.semaphore_signal(barrier, inc=1, device_id=(moved(base, offset), band), device_id_type=MESH)
    step8 = lax.broadcasted_iota(jnp.int32, (8, 128), 0).astype(F32)
    lane = lax.broadcasted_iota(jnp.int32, (32, 128), 1)
    taper_ref[...] = spread(taper_in_ref[...], tile_at_ref[...])
    scale = spread(jnp.broadcast_to(chan_ref[...], (8, 16)), chan_at_ref[...])[0:1] * (1.0 / TILE)
    cell = cell_ref[...]
    ids_ref[...] = (cell >> 3) * K_TILES + owner_ref[...] * 8 + (cell & 7)
    for side in range(2):
        places_ref[side] = spread(coords_ref[side].T, time_ref[...]) * scale
    def one(s):
        def phases(side):
            row = pl.ds(s, 1)
            turns = places_ref[side, row, :] * step8
            w = [jnp.broadcast_to(w_ref[side, i, row, :], (8, 128)) for i in range(4)]
            return powers(cos_sin_turns(turns), (w[0], w[1]), (w[2], w[3]))

        x_side = phases(0)
        y_side = phases(1)
        vr = jnp.broadcast_to(vis_ref[s, 0:1, :], (8, 128))
        vi = jnp.broadcast_to(vis_ref[s, 1:2, :], (8, 128))
        l_re = jnp.concatenate([vr * c - vi * s for c, s in y_side], 0)
        l_im = jnp.concatenate([vr * s + vi * c for c, s in y_side], 0)
        c_x = jnp.concatenate([c for c, s in x_side], 0)
        s_x = jnp.concatenate([s for c, s in x_side], 0)
        lrh, lrl = split(l_re)
        lih, lil = split(l_im)
        ch, cl = split(c_x)
        sh, sl = split(s_x)
        left = jnp.concatenate([jnp.concatenate([lrh, lih], 1), jnp.concatenate([lrl, lil], 1)], 0)
        right_h = jnp.concatenate([jnp.concatenate([ch, -sh], 1), jnp.concatenate([sh, ch], 1)], 0)
        right_l = jnp.concatenate([jnp.concatenate([cl, -sl], 1), jnp.concatenate([sl, cl], 1)], 0)
        return left, right_h, right_l

    def body(step, carry):
        first = step * (UNIT // 2)
        for half in range(2):
            rows = pl.ds(pl.multiple_of(half * PAIRS + first, UNIT // 2), UNIT // 2)
            for side in range(2):
                c8, s8 = cos_sin_turns(places_ref[side, rows, :] * 8.0)
                w_ref[side, 0, rows, :] = c8
                w_ref[side, 1, rows, :] = s8
                w_ref[side, 2, rows, :] = c8 * c8 - s8 * s8
                w_ref[side, 3, rows, :] = 2.0 * (c8 * s8)
        pixels = []
        for pair in range(UNIT // 2):
            a, b = one(first + pair), one(PAIRS + first + pair)
            left_h = jnp.concatenate([a[0][0:32], b[0][0:32]], 0)
            left_l = jnp.concatenate([a[0][32:64], b[0][32:64]], 0)
            right_h = jnp.concatenate([a[1], b[1]], 0)
            right_l = jnp.concatenate([a[2], b[2]], 0)
            both = mm_nt(jnp.concatenate([left_h, left_l], 0), right_h)
            prod = both[0:64] + (both[64:128] + mm_nt(left_h, right_l))
            pixels.append(jnp.where(lane < 64, prod[0:32], prod[32:64]) * taper_ref[...])
        ph, pl_ = split(jnp.concatenate(pixels, 0))
        q = mm3(ph, pl_, kxh_ref[...], kxl_ref[...])
        for pair in range(UNIT // 2):
            rows = slice(pair * 32, pair * 32 + 32)
            col = jnp.concatenate([q[rows, 0:128], q[rows, 128:256]], 0)
            qh, ql = split(col)
            tile = mm3(fyh_ref[...], fyl_ref[...], qh, ql)
            out_ref[pl.ds(first + pair, 32, stride=ROWS), :] = tile
        return carry

    steps = SLOT // UNIT // SENDS

    def send(part, rows):
        for offset in OFFSETS:
            to = moved(base, offset)
            pltpu.make_async_remote_copy(
                src_ref=out_ref.at[pl.ds(pl.multiple_of(to * ROWS + part, 8), rows), :],
                dst_ref=all_ref.at[base, pl.ds(pl.multiple_of(part, 8), rows), :],
                send_sem=send_sem.at[0],
                recv_sem=recv_sem.at[0],
                device_id=(to, band),
                device_id_type=MESH,
            ).start()

    rows = PAIRS // SENDS
    lax.fori_loop(0, steps, body, 0)
    pl.semaphore_wait(barrier, len(OFFSETS))
    send(0, rows)
    for offset in OFFSETS:
        pltpu.make_async_remote_copy(
            src_ref=ids_ref,
            dst_ref=all_ids_ref.at[base],
            send_sem=send_sem.at[1],
            recv_sem=recv_sem.at[1],
            device_id=(moved(base, offset), band),
            device_id_type=MESH,
        ).start()

    def later(part, carry):
        lax.fori_loop(part * steps, part * steps + steps, body, 0)
        send(part * rows, rows)
        return carry

    lax.fori_loop(1, SENDS - 1, later, 0)
    lax.fori_loop(SLOT // UNIT - steps, SLOT // UNIT, body, 0)
    send(PAIRS - rows, rows)
    own = [
        pltpu.make_async_copy(
            out_ref.at[pl.ds(pl.multiple_of(base * ROWS, 8), PAIRS), :], all_ref.at[base], own_sem.at[0]
        ),
        pltpu.make_async_copy(ids_ref, all_ids_ref.at[base], own_sem.at[1]),
    ]
    for copy in own:
        copy.start()
    for copy in own:
        copy.wait()
    for i, ref in enumerate((all_ref, all_ids_ref)):
        arrived = ref.at[pl.ds(0, len(OFFSETS))]
        pltpu.make_async_copy(arrived, arrived, send_sem.at[i]).wait()
        pltpu.make_async_copy(arrived, arrived, recv_sem.at[i]).wait()


def grid_tables():
    span = np.arange(TILE)
    c, s = waves(span, span, TILE)
    eye2 = np.eye(2)
    fx = np.block([[c, -s], [s, c]])
    fx_turned = np.block([[-s, -c], [c, -s]])
    kx = np.concatenate([np.kron(eye2, fx), np.kron(eye2, fx_turned)], 1)
    fy = np.concatenate([c, s], 1) / (TILE * math.sqrt(128.0))
    q = np.arange(128)
    time_at = np.equal.outer(np.arange(8), q // 16)
    chan_at = np.equal.outer(np.arange(16), q % 16)
    tile_at = np.equal.outer(span, q % TILE)
    ones = tuple(t.astype(np.float32).astype(ml_dtypes.bfloat16) for t in (time_at, chan_at, tile_at))
    return ones + split_np(kx) + split_np(fy)


def row_kernel(all_ref, all_ids_ref, held_ref, in_ref, out_ref, ids_ref, load_sem, store_sem, ids_sem, *accs):
    ids_copy = pltpu.make_async_copy(all_ids_ref, ids_ref, ids_sem)
    ids_copy.start()
    sources = N_BASE // LOADS
    loads = []
    for i in range(LOADS):
        part = pl.ds(i * sources, sources)
        loads.append(
            pltpu.make_async_copy(all_ref.at[part], in_ref.at[part], load_sem.at[i])
        )
        loads[i].start()
    def clear(i, carry):
        rows = pl.ds(pl.multiple_of(i * 64, 64), 64)
        for acc in accs:
            acc[rows, :] = jnp.zeros((64, 128), F32)
        return carry

    lax.fori_loop(0, G // 64, clear, 0)
    ids_copy.wait()

    def add(src, carry):
        for t in range(PAIRS):
            row = in_ref[src, t : t + 1, :]
            for half in range(2):
                acc = accs[(2 * t + half) % CHAINS]
                at = pl.ds(ids_ref[src, half, t], 1)
                acc[at, :] = acc[at, :] + row
        return carry

    for i in range(LOADS):
        loads[i].wait()
        lax.fori_loop(i * sources, (i + 1) * sources, add, 0)

    def total(half, rows):
        parts = [acc[rows, :] for acc in accs[half::2]]
        while len(parts) > 1:
            parts = [x + y for x, y in zip(parts[::2], parts[1::2])]
        return parts[0]

    low_half = lax.broadcasted_iota(jnp.int32, (K_TILES, 128), 1) < 64

    def rows_of(pair, carry):
        one = pl.ds(pl.multiple_of(pair * K_TILES, K_TILES), K_TILES)
        two = pl.ds(pl.multiple_of((pair + 16) * K_TILES, K_TILES), K_TILES)
        a1, a2 = total(0, one), total(0, two)
        b1, b2 = total(1, one), total(1, two)
        out_ref[one, :] = jnp.where(low_half, a1, b2) + pltpu.roll(jnp.where(low_half, a2, b1), 64, 1)
        return carry

    stores = []
    pairs = 16 // LOADS
    for i in range(LOADS):
        lax.fori_loop(i * pairs, (i + 1) * pairs, rows_of, 0, unroll=2)
        part = pl.ds(i * pairs * K_TILES, pairs * K_TILES)
        stores.append(pltpu.make_async_copy(out_ref.at[part, :], held_ref.at[part, :], store_sem.at[i]))
        stores[i].start()
    for store in stores:
        store.wait()


def row_tables():
    span = np.arange(K_TILES)
    c, s = waves(span, span, K_TILES)
    e = np.concatenate([c, s], 1)
    kx = np.arange(TILE)
    tc, ts = waves(kx, span, G)
    c32, s32 = waves(kx, kx, TILE)
    f = np.kron(np.eye(4), np.block([[c32, -s32], [s32, c32]]))
    return split_np(e) + (tc.astype(np.float32), ts.astype(np.float32)) + split_np(f)


TURNS = (2, 1, 3, 0)
FAR = (2, 1, 3)


def wait_for(ref, sem):
    pltpu.make_async_copy(ref, ref, sem).wait()


def send_to(source, target, send_sem, recv_sem, device):
    pltpu.make_async_remote_copy(
        src_ref=source,
        dst_ref=target,
        send_sem=send_sem,
        recv_sem=recv_sem,
        device_id=device,
        device_id_type=MESH,
    ).start()


def exchange_kernel(
    rows_ref, reh_ref, rel_ref, rtc_ref, rts_ref, rfh_ref, rfl_ref, eh_in, el_in, tc_ref, ts_ref,
    v_ref, eh_ref, el_ref, held_ref, z_ref, out_ref, mid_ref, in_ref, load_sem, send_sem, mid_sem, recv_sem, own_sem,
):
    base, band = lax.axis_index("base"), lax.axis_index("band")
    my_x, my_y, my_core = base // 8, base // 2 % 4, base % 2
    loads = []
    for i in range(4):
        part = pl.ds(i * 4 * K_TILES, 4 * K_TILES)
        loads.append(pltpu.make_async_copy(rows_ref.at[part, :], held_ref.at[part, :], load_sem.at[i]))
        loads[i].start()
    for source, target in ((eh_in, eh_ref), (el_in, el_ref)):
        loads.append(pltpu.make_async_copy(source, target, load_sem.at[len(loads)]))
        loads[-1].start()
    barrier = pltpu.get_barrier_semaphore()
    for step in range(1, N_BAND):
        pl.semaphore_signal(barrier, inc=1, device_id=(base, (band + step) % N_BAND), device_id_type=MESH)
    for offset in OFFSETS:
        pl.semaphore_signal(barrier, inc=1, device_id=(moved(base, offset), band), device_id_type=MESH)

    quarter = lax.broadcasted_iota(jnp.int32, (8, 128), 1) // 32

    def transform(group):
        turned = [held_ref[pl.ds((4 * group + i) * K_TILES, K_TILES), :].T for i in range(4)]
        hh, hl = split(jnp.concatenate(turned, 0))
        prod = mm3(hh, hl, reh_ref[...], rel_ref[...])
        for i in range(2):
            parts = []
            for t in range(4):
                at = 256 * i + 64 * t
                re, im = prod[at : at + 32], prod[at + 32 : at + 64]
                y_re = re[:, 0:256] - im[:, 256:512]
                y_im = re[:, 256:512] + im[:, 0:256]
                parts.append(y_re * rtc_ref[...] - y_im * rts_ref[...])
                parts.append(y_re * rts_ref[...] + y_im * rtc_ref[...])
            vh, vl = split(jnp.concatenate(parts, 0))
            z = mm3(rfh_ref[...], rfl_ref[...], vh, vl)
            for half in range(2):
                for j in range(2):
                    at = pl.ds((4 * group + 2 * i + j) * Z_PITCH, 128)
                    z_ref[half, at, :] = z[128 * j : 128 * j + 128, 128 * half : 128 * half + 128]

    def blocks(part, to_y):
        def one(i, carry):
            x, core = i // 2, i % 2
            b2 = x * 8 + to_y * 2 + core
            for half in range(2):
                pieces = [z_ref[half, pl.ds(part * 8 * Z_PITCH + p * 32 + b2, 8, stride=Z_PITCH), :] for p in range(4)]
                for zq in range(4):
                    block = None
                    for p in range(4):
                        turned = pieces[p] if p == zq else pltpu.roll(pieces[p], (p - zq) * 32 % 128, 1)
                        block = turned if block is None else jnp.where(quarter == p, turned, block)
                    out_ref[x, to_y, core, half * 4 + zq, 8 * part : 8 * part + 8, :] = block
            return carry

        lax.fori_loop(0, 8, one, 0, unroll=4)

    def over_band(part, k):
        to_y = (my_y + TURNS[k]) % 4
        rows = pl.ds(8 * part, 8)
        blocks(part, to_y)
        if part + k == 0:
            pl.semaphore_wait(barrier, N_BAND - 1 + len(OFFSETS))
        if k < 3:
            band_copies(4 * part + k, (slice(None),), to_y, rows)
        else:
            band_copies(4 * part + k, [(my_x + x) % 4 for x in FAR], to_y, rows)
        if (part, k) == (1, 3):
            band_copies(8, (my_x,), to_y, pl.ds(0, 16))

    def band_copies(sem, columns, to_y, rows):
        for step in (4, 3, 5, 2, 6, 1, 7, 0):
            to = (band + step) % N_BAND
            for x in columns:
                source = out_ref.at[x, to_y, :, to, rows, :]
                target = mid_ref.at[x, to_y, :, band, rows, :]
                if step:
                    send_to(source, target, send_sem, mid_sem.at[sem], (base, to))
                else:
                    own_mid[sem].append(pltpu.make_async_copy(source, target, own_sem.at[len(started)]))
                    own_mid[sem][-1].start()
                    started.append(sem)

    def over_base(part, k):
        rows = pl.ds(8 * part, 8) if part < 2 else pl.ds(0, 16)
        sem = 4 * part + k if part < 2 else 8
        offsets = (0,) if part == 2 else range(4) if k < 3 else FAR
        to_y = (my_y + TURNS[k]) % 4
        for own in own_mid[sem]:
            own.wait()
        wait_for(out_ref.at[pl.ds(0, len(offsets)), 0, :, pl.ds(0, N_BAND - 1), rows, :], mid_sem.at[sem])
        for x in offsets:
            for core in range(2):
                held = mid_ref.at[(my_x + x) % 4, to_y, (my_core + core) % 2, :, rows, :]
                target = in_ref.at[base, :, rows, :]
                if (x, TURNS[k], core) == (0, 0, 0):
                    own = pltpu.make_async_copy(held, target, own_sem.at[13])
                    own.start()
                    own_in.append(own)
                else:
                    to = (moved(base, (x, TURNS[k], core)), band)
                    send_to(held, target, send_sem, recv_sem.at[sem], to)

    def first(k):
        if k < 4:
            for part in range(2):
                came = in_ref.at[pl.ds(0, 8 if k < 3 else 6), :, pl.ds(8 * part, 8), :]
                wait_for(came, recv_sem.at[4 * part + k])
        else:
            wait_for(in_ref.at[0], recv_sem.at[8])
            own_in[0].wait()
        from_y = (my_y - TURNS[min(k, 3)] + 4) % 4

        columns = range(4) if k < 3 else [(my_x + x) % 4 for x in (FAR if k == 3 else (0,))]
        ids = [x * 8 + from_y * 2 + core for x in columns for core in range(2)]
        lefts = []
        for j in ids:
            turned = in_ref[j].reshape(128, 128).T
            lefts.append(jnp.concatenate([turned[0:64], turned[64:128]], 1))
        dh, dl = split(jnp.concatenate(lefts, 0))
        prod = mm3(dh, dl, eh_ref[...], el_ref[...])
        for t, j in enumerate(ids):
            re, im = prod[64 * t : 64 * t + 32], prod[64 * t + 32 : 64 * t + 64]
            y_re = re[:, 0:256] - im[:, 256:512]
            y_im = re[:, 256:512] + im[:, 0:256]
            tc = tc_ref[pl.ds(j, 1), :]
            ts = ts_ref[pl.ds(j, 1), :]
            v_re = y_re * tc - y_im * ts
            v_im = y_re * ts + y_im * tc
            for half in range(2):
                lanes = slice(128 * half, 128 * half + 128)
                v_ref[half, pl.ds(j, 32, stride=PITCH), :] = v_re[:, lanes]
                v_ref[half, pl.ds(32 + j, 32, stride=PITCH), :] = v_im[:, lanes]

    own_mid, own_in, started = [[] for _ in range(9)], [], []
    for part in range(2):
        for i in range(2 * part, 2 * part + 2):
            loads[i].wait()
            transform(i)
        for k in range(4):
            over_band(part, k)
    for k in range(4):
        over_base(0, k)
    for load in loads[4:]:
        load.wait()
    over_base(1, 0)
    over_base(1, 1)
    first(0)
    over_base(1, 2)
    first(1)
    over_base(1, 3)
    first(2)
    over_base(2, 3)
    first(3)
    first(4)
    wait_for(in_ref.at[pl.ds(0, 28)], send_sem)
    wait_for(in_ref.at[pl.ds(0, 31)], send_sem)


def column_kernel(v_ref, fh_ref, fl_ref, out_ref, x_ref):
    for i in range(8):
        rows = pl.ds(PITCH * i, 64)
        vh, vl = split(jnp.concatenate([v_ref[0, rows, :], v_ref[1, rows, :]], 1))
        x = mm3(fh_ref[...], fl_ref[...], vh, vl)
        for half in range(2):
            x_ref[half, rows, :] = x[:, 128 * half : 128 * half + 128]
    for c in range(2):
        for a2 in range(TILE):
            for half in range(2):
                at = a2 * 256 + half * 128
                out_ref[c, :, at : at + 128] = x_ref[half, pl.ds(c * 32 + a2, 8, stride=PITCH), :]


def column_tables():
    zs, rp, rpp = np.arange(8), np.arange(16), np.arange(2)
    r = (rpp[:, None, None] * 16 + zs[None, :, None] * 32 + rp[None, None, :]).reshape(-1)
    span = np.arange(K_TILES)
    c, s = waves(r, span, K_TILES)
    e = np.concatenate([c, s], 1)
    ky = np.arange(TILE)
    tc, ts = waves(ky, span, G)
    c32, s32 = waves(ky, ky, TILE)
    f = np.block([[c32, -s32], [s32, c32]]) / G
    return split_np(e) + (tc.astype(np.float32), ts.astype(np.float32)) + split_np(f)


VMEM = pl.BlockSpec(memory_space=pltpu.VMEM)
HBM = pl.BlockSpec(memory_space=pl.ANY)
LIMIT = pltpu.CompilerParams(vmem_limit_bytes=56 * 2**20)


def shards(visibilities, coords, chan_scale, taper_gain, owner_base, tile_cell):
    arrived, ids = pl.pallas_call(
        grid_kernel,
        out_shape=(
            jax.ShapeDtypeStruct((N_BASE, PAIRS, 128), F32),
            jax.ShapeDtypeStruct((N_BASE, 2, PAIRS), jnp.int32),
        ),
        in_specs=[VMEM] * 13,
        out_specs=(HBM, HBM),
        scratch_shapes=[
            pltpu.VMEM((2, 4, SLOT, 128), F32),
            pltpu.VMEM((TILE * ROWS, 128), F32),
            pltpu.VMEM((2, PAIRS), jnp.int32),
            pltpu.VMEM((2, SLOT, 128), F32),
            pltpu.VMEM((TILE, 128), F32),
            pltpu.SemaphoreType.DMA((2,)),
            pltpu.SemaphoreType.DMA((2,)),
            pltpu.SemaphoreType.DMA((2,)),
        ],
        compiler_params=pltpu.CompilerParams(vmem_limit_bytes=56 * 2**20, collective_id=0, has_side_effects=True),
        name="gridding",
    )(
        visibilities,
        coords.transpose(1, 2, 0),
        chan_scale.reshape(1, 16),
        owner_base.reshape(2, PAIRS),
        tile_cell.reshape(2, PAIRS),
        taper_gain,
        *[jnp.asarray(t) for t in grid_tables()],
    )
    tables = [jnp.asarray(t) for t in column_tables()]
    row_side = [jnp.asarray(t) for t in row_tables()]
    rows = pl.pallas_call(
        row_kernel,
        out_shape=jax.ShapeDtypeStruct((G // 2, 128), F32),
        in_specs=[HBM, HBM],
        out_specs=HBM,
        scratch_shapes=[
            pltpu.VMEM((N_BASE, PAIRS, 128), F32),
            pltpu.VMEM((G // 2, 128), F32),
            pltpu.SMEM((N_BASE, 2, PAIRS), jnp.int32),
            pltpu.SemaphoreType.DMA((LOADS,)),
            pltpu.SemaphoreType.DMA((LOADS,)),
            pltpu.SemaphoreType.DMA,
            *[pltpu.VMEM((G, 128), F32)] * CHAINS,
        ],
        compiler_params=LIMIT,
        name="rows",
    )(arrived, ids)
    by_target = pltpu.VMEM((4, 4, 2, N_BAND, 16, 128), F32)
    dma = pltpu.SemaphoreType.DMA
    turned = pl.pallas_call(
        exchange_kernel,
        out_shape=jax.ShapeDtypeStruct((2, TILE * PITCH, 128), F32),
        in_specs=[HBM] + [VMEM] * 6 + [HBM] * 2 + [VMEM] * 2,
        out_specs=VMEM,
        scratch_shapes=[
            pltpu.VMEM(tables[0].shape, BF16),
            pltpu.VMEM(tables[1].shape, BF16),
            pltpu.VMEM((G // 2, 128), F32),
            pltpu.VMEM((2, 16 * Z_PITCH, 128), F32),
            by_target,
            by_target,
            pltpu.VMEM((N_BASE, N_BAND, 16, 128), F32),
            dma((6,)),
            dma,
            dma((9,)),
            dma((9,)),
            dma((14,)),
        ],
        compiler_params=pltpu.CompilerParams(vmem_limit_bytes=56 * 2**20, collective_id=1, has_side_effects=True),
        name="exchange",
    )(rows, *row_side, *tables[:4])
    return pl.pallas_call(
        column_kernel,
        out_shape=jax.ShapeDtypeStruct((2, TILE, G), F32),
        grid=(TILE // 8,),
        in_specs=[
            pl.BlockSpec((2, 8 * PITCH, 128), lambda i: (0, i, 0)),
            pl.BlockSpec((64, 64), lambda i: (0, 0)),
            pl.BlockSpec((64, 64), lambda i: (0, 0)),
        ],
        out_specs=pl.BlockSpec((2, 8, G), lambda i: (0, i, 0)),
        scratch_shapes=[pltpu.VMEM((2, 8 * PITCH, 128), F32)],
        compiler_params=LIMIT,
        name="columns",
    )(turned, *tables[4:])


def solution(mesh):
    placed = (
        P(("base", "band"), None, None),
        P(("base", "band"), None, None),
        P(),
        P(),
        P(("base", "band"), None),
        P(("base", "band")),
    )
    return jax.shard_map(
        shards,
        mesh=mesh,
        in_specs=placed,
        out_specs=P(None, ("base", "band"), None),
        check_vma=False,
    )
```
